32 devices in a mesh: groups: 2 (over y), dp: 4 (over z), vocab: 4 (over x, core).
Axes of the slice: x: 2, y: 2, z: 4, core: 2. Of those that a mesh axis runs over, the one named last changes fastest.
Arguments:
- tokens_in: bfloat16 [128, 3584], P(('groups', 'dp')), parts along dimension 0, may hold values from -6 to 6
- attention: bfloat16 [128, 4096], P(('groups', 'dp'), 'vocab'), parts along dimension 0, may hold values from -6 to 6
- out_projection: bfloat16 [4096, 3584], P('vocab', 'dp'), may hold values from -0.09375 to 0.09375
- tangent: float32 [8192, 3584], P(('groups', 'vocab'), 'dp'), parts along dimension 0, may hold values from -0.09375 to 0.09375
- norm_gain: bfloat16 [3584], replicated, may hold values from 0.25 to 1.75
- head_weight: bfloat16 [3584, 8192], P(None, ('dp', 'vocab')), may hold values from -1 to 1
- lengths: int32 [8], P('groups'), parts along dimension 0, may hold values from 1 to 16, 32 in all
- sampled: int32 [128], P('groups'), parts along dimension 0, may hold values from 0 to 8191
Outputs:
- fisher_product: float32 [8192, 3584], P(('groups', 'vocab'), 'dp'), parts along dimension 0
- token_tangent: float32 [64], P(('groups', 'dp')), parts along dimension 0
The draws below stay inside these ranges and needn't reach their ends.
There are 2 independent parts, one for each index of `groups`. The reference program is written for one: setup_inputs(seed, part) draws one part's arguments, and reference() takes and returns one part's arrays. A program takes and returns all parts, laid end to end along the dimension named above; an argument that names none is the same for every part. Nothing has to cross between parts.
Inputs may be any that keep to these rules, and one draw needn't show every extreme that they name: Slots 0 to lengths[i] - 1 of dp block i are live; the entries sum to 32.
All inputs are finite; a program needn't handle non-finite values.
Results may differ from the reference program's by a relative error of at most 0.0096.
Values may be sent and summed in bfloat16 or wider, within the bound.
A program may use at most 128 MiB of HBM per device.

```python
import math
import jax
import jax.numpy as jnp
import numpy as np
from jax import lax

D = 3584
Q = 4096
TOK_DEV = 16
TOKENS = 64
LIVE = 32
VOCAB = 8192
N_DP = 4


def with_ends(drawn, key, least, largest):
    dims = drawn.shape
    index_at = [jax.random.randint(jax.random.fold_in(key, axis), (), 0, dims[axis]) for axis in range(len(dims))]
    drawn = drawn.at[tuple(index_at)].set(least)
    longest = dims.index(max(dims))
    index_at[longest] = (index_at[longest] + 1) % dims[longest]
    return drawn.at[tuple(index_at)].set(largest)


def levels(own_key, dims, pieces, low, top_value):
    level = 1.0
    for axis_at, parts in pieces:
        draws = jax.random.uniform(jax.random.fold_in(jax.random.fold_in(own_key, 6), axis_at), (parts,), jnp.float32, low / len(pieces), top_value / len(pieces))
        level = level * jnp.repeat(jnp.exp(draws), dims[axis_at] // parts).reshape((-1,) + (1,) * (len(dims) - 1 - axis_at))
    return level


def rank_bounds(amount, lean):
    portions = [(1 << 20) // math.isqrt(grade ** lean) + 1 for grade in range(1, amount + 1)]
    scale = 1 + sum(portions) // (1 << 30)
    return np.cumsum(np.array([max(1, weight // scale) for weight in portions]))


def ranked_ids(own_key, dims, amount, slope):
    listing = rank_bounds(amount, slope)
    pick = jax.random.randint(jax.random.fold_in(own_key, 1), dims, 0, int(listing[amount - 1]))
    rank = jnp.searchsorted(jnp.asarray(listing, jnp.int32), pick, side="right")
    return jax.random.permutation(jax.random.fold_in(own_key, 2), amount)[rank].astype(jnp.int32)


def split_up(amount, total, limit, lean):
    portions = [(1 << 20) // math.isqrt(rank ** lean) + 1 for rank in range(2, amount + 1)]
    rest, holding = total - limit - (amount - 1), [1] * (amount - 1)
    while rest > 0:
        free = [i for i in range(amount - 1) if holding[i] < limit]
        mass, budget = sum([portions[i] for i in free]), rest
        for i in free:
            more = min(limit - holding[i], max(1, budget * portions[i] // mass), rest)
            holding[i] = holding[i] + more
            rest = rest - more
    return np.array([limit] + holding)


def uneven(key, number_of, total, most, skew):
    if number_of == 2:
        one = jax.random.randint(key, (), max(1, total - most), min(most, total - 1) + 1)
        return jnp.stack([one, total - one])
    sizes = jnp.asarray(split_up(number_of, total, most, skew), jnp.int32)
    twos = (number_of - 1) // 2
    giver, taker = sizes[1:1 + 2 * twos:2], sizes[2:2 + 2 * twos:2]
    margin = jnp.minimum(giver - 1, most - taker)
    passed = jax.random.randint(jax.random.fold_in(key, 1), (twos,), 0, 1 << 20) % (margin + 1)
    sizes = sizes.at[1:1 + 2 * twos:2].set(giver - passed).at[2:2 + 2 * twos:2].set(taker + passed)
    return sizes[jax.random.permutation(jax.random.fold_in(key, 2), number_of)]


def gaussian(stream_key, shape, deviation, bound, pieces=(), held_as=jnp.bfloat16):
    drawn = jax.random.normal(stream_key, shape, jnp.float32) * deviation
    if len(pieces) > 0:
        drawn = levels(stream_key, shape, pieces, -0.22, 0.18) * drawn
    return jnp.clip(drawn, min=-bound, max=bound).astype(held_as)


def setup_inputs(seed: int = 0, part: int = 0) -> dict:
    splits = jax.random.split(jax.random.key(seed), 9)
    own_keys = jax.random.split(jax.random.fold_in(splits[8], part), 9)
    return {
        "tokens_in": gaussian(own_keys[0], (TOKENS, D), 1.0, 6.0, ((0, 4),)),
        "attention": gaussian(own_keys[1], (TOKENS, Q), 1.0, 6.0, ((0, 4), (1, 4))),
        "out_projection": gaussian(splits[2], (Q, D), Q ** -0.5, 0.09375, ((0, 4), (1, 4))),
        "tangent": gaussian(own_keys[3], (Q, D), Q ** -0.5, 0.09375, ((0, 4), (1, 4)), jnp.float32),
        "norm_gain": jnp.clip(1.0 + 0.15 * jax.random.normal(splits[4], (D,), jnp.float32), 0.25, 1.75).astype(jnp.bfloat16),
        "head_weight": gaussian(splits[5], (D, VOCAB), 0.067, 1.0, ((1, 16),)),
        "lengths": uneven(own_keys[6], N_DP, LIVE, TOK_DEV, 2).astype(jnp.int32),
        "sampled": with_ends(ranked_ids(own_keys[7], (TOKENS,), VOCAB, 2), jax.random.fold_in(own_keys[7], 3), 0, VOCAB - 1).astype(jnp.int32),
    }


SOFT_CAP = 30.0
EPSILON = 1e-06

def packed_slots(lengths, slot_count, total_live):
    lengths = lengths.astype(jnp.int32)
    block_ends = jnp.cumsum(lengths).astype(jnp.int32)
    block_starts = (block_ends - lengths).astype(jnp.int32)
    packed = jnp.arange(total_live, dtype=jnp.int32)
    owners = lax.optimization_barrier(jnp.sum((block_ends[None, :] <= packed[:, None]).astype(jnp.int32), axis=1)).astype(jnp.int32)
    owner_hits = owners[:, None] == jnp.arange(lengths.shape[0], dtype=jnp.int32)[None, :]
    first_slot = lax.optimization_barrier(jnp.sum(jnp.where(owner_hits, block_starts[None, :], 0), axis=1)).astype(jnp.int32)
    local_slot = (packed - first_slot).astype(jnp.int32)
    return (owners, local_slot, (owners * slot_count + local_slot).astype(jnp.int32))

def reference(tokens_in, attention, out_projection, tangent, norm_gain, head_weight, lengths, sampled):
    slots_all = tokens_in.shape[0]
    slot_ids = jnp.arange(slots_all, dtype=jnp.int32)
    per_slot = jnp.repeat(lengths.astype(jnp.int32), TOK_DEV, total_repeat_length=slots_all)
    weight = (slot_ids % TOK_DEV < per_slot).astype(jnp.float32)
    tangent_narrow = tangent.astype(jnp.bfloat16)
    hidden = tokens_in.astype(jnp.float32) + jnp.dot(attention, out_projection, preferred_element_type=jnp.float32)
    tangent_hidden = jnp.dot(attention, tangent_narrow, preferred_element_type=jnp.float32)
    gain_wide = norm_gain.astype(jnp.float32)
    scale_row = lax.rsqrt(lax.optimization_barrier(jnp.mean(hidden * hidden, axis=1, keepdims=True)) + EPSILON)
    normed = (gain_wide * hidden * scale_row).astype(jnp.bfloat16)
    inner_dot = lax.optimization_barrier(jnp.mean(hidden * tangent_hidden, axis=1, keepdims=True))
    tangent_normed = (gain_wide * scale_row * (tangent_hidden - hidden * scale_row * scale_row * inner_dot)).astype(jnp.bfloat16)
    logits = jnp.dot(normed, head_weight, preferred_element_type=jnp.float32)
    tangent_logits = jnp.dot(tangent_normed, head_weight, preferred_element_type=jnp.float32)
    squashed = jnp.tanh(logits / SOFT_CAP)
    capped = SOFT_CAP * squashed
    slopes = 1.0 - squashed * squashed
    tangent_capped = slopes * tangent_logits
    exp_values = jnp.exp(capped)
    totals = lax.optimization_barrier(jnp.sum(exp_values, axis=1))
    tangent_mean = lax.optimization_barrier(jnp.sum(exp_values * tangent_capped, axis=1)) / totals
    picked = jnp.take_along_axis(tangent_capped, sampled.astype(jnp.int32)[:, None], axis=1)[:, 0]
    back_logits = (weight[:, None] * exp_values / totals[:, None] * (tangent_capped - tangent_mean[:, None]) * slopes).astype(jnp.bfloat16)
    back_normed = jnp.dot(back_logits, head_weight.T, preferred_element_type=jnp.float32)
    back_gain = gain_wide * back_normed
    inner_back = lax.optimization_barrier(jnp.mean(hidden * back_gain, axis=1, keepdims=True))
    back_hidden = (scale_row * back_gain - hidden * scale_row * scale_row * scale_row * inner_back).astype(jnp.bfloat16)
    fisher_product = jnp.dot(attention.T, back_hidden, preferred_element_type=jnp.float32)
    owners, local_slot, packed_slot = packed_slots(lengths, TOK_DEV, LIVE)
    token_tangent = jnp.take(picked - tangent_mean, packed_slot)
    return (fisher_product, token_tangent)
```

```python
import functools

import jax
import jax.numpy as jnp
from jax import lax
from jax.experimental import pallas as pl
from jax.experimental.pallas import tpu as pltpu
from jax.sharding import PartitionSpec as P

SOFT_CAP = 30.0
EPSILON = 1e-06
MESH = pl.DeviceIdType.MESH
LANES = 128
ROWS = 8
F32 = jnp.float32
BF16 = jnp.bfloat16
HIGHEST = lax.Precision.HIGHEST
NT = (((1,), (1,)), ((), ()))


def fused_kernel(
    n_dp, n_vocab,
    lengths_ref, sampled_ref, gain_ref, tokens_hbm, attention_hbm, projection_hbm, tangent_hbm, head_hbm,
    packed_ref, back_ref, token_ref,
    tokens_own, tokens_send, tokens_all, attention_all, projection, tangent, tangent_narrow, head,
    hid_send, hid_all, tan_send, tan_all, norm_all, msg_all, stat_all, part_send, part_all, bh_all,
    local_sem, att_s, att_r, tok_s, tok_r, hid_s, hid_r, tan_s, tan_r, norm_s, norm_r,
    msg_s, msg_r, stat_s, stat_r, part_s, part_r, bh_s, bh_r,
):
    d, v = lax.axis_index("dp"), lax.axis_index("vocab")
    n_all = n_dp * n_vocab
    me = d * n_vocab + v
    slots = tokens_all.shape[1]
    wide = tokens_all.shape[2]
    live = n_vocab * ROWS
    model = wide * n_dp
    columns = head.shape[1]
    base = part_all.shape[2] - LANES

    loads = [
        pltpu.make_async_copy(attention_hbm, attention_all.at[d], local_sem.at[0]),
        pltpu.make_async_copy(tokens_hbm, tokens_own, local_sem.at[1]),
        pltpu.make_async_copy(projection_hbm, projection, local_sem.at[2]),
        pltpu.make_async_copy(tangent_hbm, tangent, local_sem.at[3]),
        pltpu.make_async_copy(head_hbm, head, local_sem.at[4]),
    ]
    for load in loads:
        load.start()

    def peer_of(step):
        peer = lax.rem(me + step, n_all)
        return peer, lax.div(peer, n_vocab), lax.rem(peer, n_vocab)

    barrier = pltpu.get_barrier_semaphore()

    @pl.loop(1, n_all)
    def _(step):
        _, pd, pv = peer_of(step)
        pl.semaphore_signal(barrier, inc=1, device_id={"dp": pd, "vocab": pv}, device_id_type=MESH)

    pl.semaphore_wait(barrier, n_all - 1)

    def along_dp(step):
        return lax.rem(d + step, n_dp)

    def att_copy(step):
        return pltpu.make_async_remote_copy(
            attention_hbm, attention_all.at[d], att_s.at[step], att_r.at[step],
            device_id={"dp": along_dp(step)}, device_id_type=MESH)

    def tok_copy(step):
        return pltpu.make_async_remote_copy(
            tokens_send.at[along_dp(step)], tokens_all.at[d], tok_s.at[step], tok_r.at[step],
            device_id={"dp": along_dp(step)}, device_id_type=MESH)

    for step in range(1, n_dp):
        att_copy(step).start()
    loads[1].wait()
    for block in range(n_dp):
        tokens_send[block] = tokens_own[:, block * wide : (block + 1) * wide]
    for step in range(1, n_dp):
        tok_copy(step).start()
    tokens_all[d] = tokens_send[d]

    slot_at = lax.broadcasted_iota(jnp.int32, (live, n_dp * slots), 1)
    row_at = lax.broadcasted_iota(jnp.int32, (live, n_dp * slots), 0)
    hit = jnp.zeros((live, n_dp * slots), jnp.bool_)
    start = jnp.int32(0)
    for block in range(n_dp):
        length = lengths_ref[block]
        place = slot_at - block * slots
        hit = hit | ((place >= 0) & (place < length) & (row_at == start + place))
        start = start + length
    pick = jnp.where(hit, 1.0, 0.0)
    pick_narrow = pick.astype(BF16)
    wanted = jnp.sum(pick * sampled_ref[...].astype(F32), axis=1, keepdims=True).astype(jnp.int32)

    gain = jnp.zeros((1, wide), F32)
    for block in range(n_dp):
        gain = jnp.where(d == block, gain_ref[:, block * wide : (block + 1) * wide].astype(F32), gain)

    loads[3].wait()
    tangent_narrow[...] = tangent[...].astype(BF16)
    loads[2].wait()
    loads[0].wait()
    for step in range(1, n_dp):
        att_copy(step).wait()
    everything = attention_all[...].reshape(n_dp * slots, attention_all.shape[2])
    packed = jnp.dot(pick_narrow, everything, preferred_element_type=F32).astype(BF16)
    packed_ref[...] = packed

    def along_vocab(step):
        return lax.rem(v + step, n_vocab)

    def chunk_copy(src, dst, send, recv):
        def copy(step):
            return pltpu.make_async_remote_copy(
                src.at[along_vocab(step)], dst.at[v], send.at[step], recv.at[step],
                device_id={"vocab": along_vocab(step)}, device_id_type=MESH)

        return copy

    hid_copy = chunk_copy(hid_send, hid_all, hid_s, hid_r)
    tan_copy = chunk_copy(tan_send, tan_all, tan_s, tan_r)
    hid_send[...] = jnp.dot(packed, projection[...], preferred_element_type=F32).reshape(n_vocab, ROWS, wide)
    for step in range(1, n_vocab):
        hid_copy(step).start()
    hid_all[v] = hid_send[v]
    tan_send[...] = jnp.dot(packed, tangent_narrow[...], preferred_element_type=F32).reshape(n_vocab, ROWS, wide)
    for step in range(1, n_vocab):
        tan_copy(step).start()
    tan_all[v] = tan_send[v]

    for step in range(1, n_dp):
        tok_copy(step).wait()
    my_slot = lax.broadcasted_iota(jnp.int32, (ROWS, live), 1)
    my_row = lax.broadcasted_iota(jnp.int32, (ROWS, live), 0) + v * ROWS
    own_rows = jnp.where(my_slot == my_row, 1.0, 0.0)
    own_pick = jnp.dot(own_rows.astype(BF16), pick_narrow, preferred_element_type=F32).astype(BF16)
    tokens = jnp.dot(
        own_pick, tokens_all[...].reshape(n_dp * slots, wide), preferred_element_type=F32
    )
    for step in range(1, n_vocab):
        hid_copy(step).wait()
    hidden = tokens + jnp.sum(hid_all[...], axis=0)
    for step in range(1, n_vocab):
        tan_copy(step).wait()
    tangent_hidden = jnp.sum(tan_all[...], axis=0)

    lane = lax.broadcasted_iota(jnp.int32, (ROWS, LANES), 1)
    squares = jnp.sum(hidden * hidden, axis=1, keepdims=True)
    cross = jnp.sum(hidden * tangent_hidden, axis=1, keepdims=True)
    norm_all[d] = jnp.where(lane < 1, squares, cross)

    def norm_copy(step):
        return pltpu.make_async_remote_copy(
            norm_all.at[d], norm_all.at[d], norm_s.at[step], norm_r.at[step],
            device_id={"dp": along_dp(step)}, device_id_type=MESH)

    for step in range(1, n_dp):
        norm_copy(step).start()
    for step in range(1, n_dp):
        norm_copy(step).wait()
    inverse = 1.0 / model
    means = jnp.sum(norm_all[...], axis=0) * inverse
    scale = lax.rsqrt(means[:, 0:1] + EPSILON)
    normed = gain * hidden * scale
    tangent_normed = gain * scale * (tangent_hidden - hidden * scale * scale * means[:, 1:2])
    msg_all[me] = jnp.concatenate([normed, tangent_normed], axis=0).astype(BF16)

    def to_all(src, dst, send, recv):
        def copy(step):
            _, pd, pv = peer_of(step)
            return pltpu.make_async_remote_copy(
                src(step), dst.at[me], send.at[step], recv.at[step],
                device_id={"dp": pd, "vocab": pv}, device_id_type=MESH)

        return copy

    def start_all(copy):
        @pl.loop(1, n_all)
        def _(step):
            copy(step).start()

    def wait_all(copy):
        @pl.loop(1, n_all)
        def _(step):
            copy(step).wait()

    msg_copy = to_all(lambda step: msg_all.at[me], msg_all, msg_s, msg_r)
    start_all(msg_copy)
    loads[4].wait()
    wait_all(msg_copy)

    pair = jnp.zeros((n_vocab * 2 * ROWS, columns), F32)
    for block in range(n_dp):
        pair = pair + jnp.dot(
            msg_all[block * n_vocab : (block + 1) * n_vocab].reshape(n_vocab * 2 * ROWS, wide),
            head[block * wide : (block + 1) * wide, :],
            preferred_element_type=F32,
        )
    pair = pair.reshape(n_vocab, 2 * ROWS, columns)
    logits = pair[:, 0:ROWS].reshape(live, columns)
    squashed = jnp.tanh(logits * (1.0 / SOFT_CAP))
    slopes = 1.0 - squashed * squashed
    tangent_capped = slopes * pair[:, ROWS:].reshape(live, columns)
    exp_values = jnp.exp(SOFT_CAP * squashed)
    column_at = lax.broadcasted_iota(jnp.int32, (live, columns), 1) + me * columns
    total = jnp.sum(exp_values, axis=1, keepdims=True)
    weighted = jnp.sum(exp_values * tangent_capped, axis=1, keepdims=True)
    picked = jnp.sum(jnp.where(column_at == wanted, tangent_capped, 0.0), axis=1, keepdims=True)
    stat_lane = lax.broadcasted_iota(jnp.int32, (live, LANES), 1)
    stats = (
        jnp.where(stat_lane == 0, total, 0.0)
        + jnp.where(stat_lane == 1, weighted, 0.0)
        + jnp.where(stat_lane == 2, picked, 0.0)
    )
    turn = jnp.where(
        lax.broadcasted_iota(jnp.int32, (ROWS, LANES), 0) == lax.broadcasted_iota(jnp.int32, (ROWS, LANES), 1), 1.0, 0.0
    )
    stat_all[me, :, 0:live] = lax.dot_general(turn, stats, NT, precision=HIGHEST, preferred_element_type=F32)
    if live < LANES:
        stat_all[me, :, live:] = jnp.zeros((ROWS, LANES - live), F32)
    stat_copy = to_all(lambda step: stat_all.at[me], stat_all, stat_s, stat_r)
    start_all(stat_copy)
    wait_all(stat_copy)
    across = jnp.sum(stat_all[...], axis=0)
    across = across[:, 0:live]
    mean_row = across[1:2] / across[0:1]
    token_ref[...] = across[2:3] - mean_row
    both = jnp.where(lax.broadcasted_iota(jnp.int32, (ROWS, live), 0) == 0, across[0:1], mean_row)
    square = jnp.where(
        lax.broadcasted_iota(jnp.int32, (live, live), 0) == lax.broadcasted_iota(jnp.int32, (live, live), 1), 1.0, 0.0
    )
    down = lax.dot_general(square, both, NT, precision=HIGHEST, preferred_element_type=F32)
    all_total, tangent_mean = down[:, 0:1], down[:, 1:2]

    back_logits = (exp_values / all_total * (tangent_capped - tangent_mean) * slopes).astype(BF16)
    inner_part = jnp.sum(back_logits.astype(F32) * logits, axis=1, keepdims=True)
    inner_tail = jnp.where(stat_lane == 0, inner_part, 0.0).reshape(n_vocab, ROWS, LANES)
    for block in range(n_dp):
        part_send[block * n_vocab : (block + 1) * n_vocab, :, 0:wide] = lax.dot_general(
            back_logits, head[block * wide : (block + 1) * wide, :], NT, preferred_element_type=F32
        ).reshape(n_vocab, ROWS, wide)
        part_send[block * n_vocab : (block + 1) * n_vocab, :, base:] = inner_tail

    def part_src(step):
        peer, _, _ = peer_of(step)
        return part_send.at[peer]

    part_copy = to_all(part_src, part_all, part_s, part_r)
    start_all(part_copy)
    part_all[me] = part_send[me]
    wait_all(part_copy)
    back_gain = gain * jnp.sum(part_all[:, :, 0:wide], axis=0)
    inner_back = jnp.sum(jnp.sum(part_all[:, :, base:], axis=0), axis=1, keepdims=True) * inverse
    bh_all[v] = scale * back_gain - hidden * (scale * scale * inner_back)

    def bh_copy(step):
        return pltpu.make_async_remote_copy(
            bh_all.at[v], bh_all.at[v], bh_s.at[step], bh_r.at[step],
            device_id={"vocab": along_vocab(step)}, device_id_type=MESH)

    for step in range(1, n_vocab):
        bh_copy(step).start()
    for step in range(1, n_vocab):
        bh_copy(step).wait()
    back_ref[...] = bh_all[...].reshape(live, wide).astype(BF16)


def local(n_dp, n_vocab, tokens_in, attention, out_projection, tangent, norm_gain, head_weight, lengths, sampled):
    slots, model = tokens_in.shape
    features, wide = out_projection.shape
    columns = head_weight.shape[1]
    live_dev = slots // 2
    live = live_dev * n_dp
    assert live == n_vocab * ROWS and live <= LANES
    n_all = n_dp * n_vocab
    padded = -(-wide // LANES) * LANES + LANES
    vmem, anywhere = pl.BlockSpec(memory_space=pltpu.VMEM), pl.BlockSpec(memory_space=pl.ANY)
    dma = pltpu.SemaphoreType.DMA
    packed, back, token_all = pl.pallas_call(
        functools.partial(fused_kernel, n_dp, n_vocab),
        out_shape=(
            jax.ShapeDtypeStruct((live, features), BF16),
            jax.ShapeDtypeStruct((live, wide), BF16),
            jax.ShapeDtypeStruct((1, live), F32),
        ),
        in_specs=[pl.BlockSpec(memory_space=pltpu.SMEM), vmem, vmem] + [anywhere] * 5,
        out_specs=(vmem, vmem, vmem),
        scratch_shapes=[
            pltpu.VMEM((slots, model), BF16),
            pltpu.VMEM((n_dp, slots, wide), BF16),
            pltpu.VMEM((n_dp, slots, wide), BF16),
            pltpu.VMEM((n_dp, slots, features), BF16),
            pltpu.VMEM((features, wide), BF16),
            pltpu.VMEM((features, wide), F32),
            pltpu.VMEM((features, wide), BF16),
            pltpu.VMEM((model, columns), BF16),
            pltpu.VMEM((n_vocab, ROWS, wide), F32),
            pltpu.VMEM((n_vocab, ROWS, wide), F32),
            pltpu.VMEM((n_vocab, ROWS, wide), F32),
            pltpu.VMEM((n_vocab, ROWS, wide), F32),
            pltpu.VMEM((n_dp, ROWS, LANES), F32),
            pltpu.VMEM((n_all, 2 * ROWS, wide), BF16),
            pltpu.VMEM((n_all, ROWS, LANES), F32),
            pltpu.VMEM((n_all, ROWS, padded), F32),
            pltpu.VMEM((n_all, ROWS, padded), F32),
            pltpu.VMEM((n_vocab, ROWS, wide), F32),
            dma((5,)),
            dma((n_dp,)), dma((n_dp,)), dma((n_dp,)), dma((n_dp,)),
            dma((n_vocab,)), dma((n_vocab,)), dma((n_vocab,)), dma((n_vocab,)),
            dma((n_dp,)), dma((n_dp,)),
            dma((n_all,)), dma((n_all,)), dma((n_all,)), dma((n_all,)), dma((n_all,)), dma((n_all,)),
            dma((n_vocab,)), dma((n_vocab,)),
        ],
        compiler_params=pltpu.CompilerParams(
            collective_id=0, has_side_effects=True, vmem_limit_bytes=40 * 1024 * 1024
        ),
    )(lengths, sampled.reshape(1, -1), norm_gain.reshape(1, -1),
      tokens_in, attention, out_projection, tangent, head_weight)
    fisher_product = lax.dot_general(packed, back, (((0,), (0,)), ((), ())), preferred_element_type=F32)
    token_mine = lax.dynamic_slice_in_dim(token_all[0], lax.axis_index("dp") * live_dev, live_dev)
    return (fisher_product, token_mine)


def solution(mesh):
    return jax.shard_map(
        functools.partial(local, mesh.shape["dp"], mesh.shape["vocab"]),
        mesh=mesh,
        in_specs=(
            P(("groups", "dp"), None),
            P(("groups", "dp"), "vocab"),
            P("vocab", "dp"),
            P(("groups", "vocab"), "dp"),
            P(),
            P(None, ("dp", "vocab")),
            P("groups"),
            P("groups"),
        ),
        out_specs=(P(("groups", "vocab"), "dp"), P(("groups", "dp"))),
        check_vma=False,
    )
```

```python
import functools

import jax
import jax.numpy as jnp
from jax import lax
from jax.experimental import pallas as pl
from jax.experimental.pallas import tpu as pltpu
from jax.sharding import PartitionSpec as P

SOFT_CAP = 30.0
EPSILON = 1e-06
MESH = pl.DeviceIdType.MESH
LANES = 128
ROWS = 8
F32 = jnp.float32
BF16 = jnp.bfloat16
NT = (((1,), (1,)), ((), ()))


def fused_kernel(
    n_dp, n_vocab,
    lengths_hbm, sampled_hbm, gain_hbm, tokens_hbm, attention_hbm, projection_hbm, tangent_hbm, head_hbm,
    packed_ref, back_ref, token_ref,
    lengths_ref, sampled_ref, gain_ref, tokens_own, tokens_send, tokens_all, attention_all, projection, tangent, tangent_narrow, head,
    hid_send, hid_all, tan_send, tan_all, norm_all, msg_all, stat_all, part_send, part_all, bh_all,
    local_sem, att_s, att_r, tok_s, tok_r, hid_s, hid_r, tan_s, tan_r, norm_s, norm_r,
    msg_s, msg_r, pass_s, pass_r, stat_s, stat_r, part_s, part_r, bh_s, bh_r,
):
    d, v = lax.axis_index("dp"), lax.axis_index("vocab")
    n_all = n_dp * n_vocab
    me = d * n_vocab + v
    slots = tokens_all.shape[1]
    wide = tokens_all.shape[2]
    live = n_vocab * ROWS
    model = wide * n_dp
    columns = head.shape[1]
    base = part_all.shape[2] - LANES

    loads = [
        pltpu.make_async_copy(attention_hbm, attention_all.at[d], local_sem.at[0]),
        pltpu.make_async_copy(tokens_hbm, tokens_own, local_sem.at[1]),
        pltpu.make_async_copy(projection_hbm, projection, local_sem.at[2]),
        pltpu.make_async_copy(tangent_hbm, tangent, local_sem.at[3]),
        pltpu.make_async_copy(lengths_hbm, lengths_ref, local_sem.at[5]),
        pltpu.make_async_copy(sampled_hbm, sampled_ref, local_sem.at[6]),
        pltpu.make_async_copy(gain_hbm, gain_ref, local_sem.at[7]),
        pltpu.make_async_copy(head_hbm, head, local_sem.at[4]),
    ]
    for load in loads:
        load.start()

    def peer_of(step):
        peer = lax.rem(me + step, n_all)
        return peer, lax.div(peer, n_vocab), lax.rem(peer, n_vocab)

    def along_dp(step):
        return lax.rem(d + step, n_dp)

    def along_vocab(step):
        return lax.rem(v + step, n_vocab)

    barrier = pltpu.get_barrier_semaphore()
    for step in range(1, n_dp):
        pl.semaphore_signal(barrier, inc=1, device_id={"dp": along_dp(step)}, device_id_type=MESH)
    for step in range(1, n_vocab):
        pl.semaphore_signal(barrier, inc=1, device_id={"vocab": along_vocab(step)}, device_id_type=MESH)
    pl.semaphore_wait(barrier, n_dp + n_vocab - 2)

    def att_copy(step):
        return pltpu.make_async_remote_copy(
            attention_hbm, attention_all.at[d], att_s.at[step], att_r.at[step],
            device_id={"dp": along_dp(step)}, device_id_type=MESH)

    def tok_copy(step):
        return pltpu.make_async_remote_copy(
            tokens_send.at[along_dp(step)], tokens_all.at[d], tok_s.at[step], tok_r.at[step],
            device_id={"dp": along_dp(step)}, device_id_type=MESH)

    for step in range(1, n_dp):
        att_copy(step).start()
    loads[1].wait()
    for block in range(n_dp):
        tokens_send[block] = tokens_own[:, block * wide : (block + 1) * wide]
    for step in range(1, n_dp):
        tok_copy(step).start()
    tokens_all[d] = tokens_send[d]

    for load in loads[4:7]:
        load.wait()

    slot_at = lax.broadcasted_iota(jnp.int32, (live, n_dp * slots), 1)
    row_at = lax.broadcasted_iota(jnp.int32, (live, n_dp * slots), 0)
    hit = jnp.zeros((live, n_dp * slots), jnp.bool_)
    start = jnp.int32(0)
    for block in range(n_dp):
        length = lengths_ref[block]
        place = slot_at - block * slots
        hit = hit | ((place >= 0) & (place < length) & (row_at == start + place))
        start = start + length
    pick = jnp.where(hit, 1.0, 0.0)
    pick_narrow = pick.astype(BF16)
    wanted = jnp.sum(pick * sampled_ref[...].astype(F32), axis=1, keepdims=True).astype(jnp.int32)

    gain = jnp.zeros((1, wide), F32)
    for block in range(n_dp):
        gain = jnp.where(d == block, gain_ref[:, block * wide : (block + 1) * wide].astype(F32), gain)

    loads[3].wait()
    tangent_narrow[...] = tangent[...].astype(BF16)
    loads[2].wait()
    loads[0].wait()
    for step in range(1, n_dp):
        att_copy(step).wait()
    everything = attention_all[...].reshape(n_dp * slots, attention_all.shape[2])
    packed = jnp.dot(pick_narrow, everything, preferred_element_type=F32).astype(BF16)
    packed_ref[...] = packed

    def chunk_copy(src, dst, send, recv):
        def copy(step):
            return pltpu.make_async_remote_copy(
                src.at[along_vocab(step)], dst.at[v], send.at[step], recv.at[step],
                device_id={"vocab": along_vocab(step)}, device_id_type=MESH)

        return copy

    hid_copy = chunk_copy(hid_send, hid_all, hid_s, hid_r)
    tan_copy = chunk_copy(tan_send, tan_all, tan_s, tan_r)
    hid_send[...] = jnp.dot(packed, projection[...], preferred_element_type=F32).reshape(n_vocab, ROWS, wide)
    for step in range(1, n_vocab):
        hid_copy(step).start()
    hid_all[v] = hid_send[v]
    tan_send[...] = jnp.dot(packed, tangent_narrow[...], preferred_element_type=F32).reshape(n_vocab, ROWS, wide)
    for step in range(1, n_vocab):
        tan_copy(step).start()
    tan_all[v] = tan_send[v]

    for step in range(1, n_dp):
        tok_copy(step).wait()
    my_slot = lax.broadcasted_iota(jnp.int32, (ROWS, live), 1)
    my_row = lax.broadcasted_iota(jnp.int32, (ROWS, live), 0) + v * ROWS
    own_rows = jnp.where(my_slot == my_row, 1.0, 0.0)
    own_pick = jnp.dot(own_rows.astype(BF16), pick_narrow, preferred_element_type=F32).astype(BF16)
    tokens = jnp.dot(
        own_pick, tokens_all[...].reshape(n_dp * slots, wide), preferred_element_type=F32
    )
    for step in range(1, n_vocab):
        hid_copy(step).wait()
    hidden = tokens + jnp.sum(hid_all[...], axis=0)
    for step in range(1, n_vocab):
        tan_copy(step).wait()
    tangent_hidden = jnp.sum(tan_all[...], axis=0)

    lane = lax.broadcasted_iota(jnp.int32, (ROWS, LANES), 1)
    squares = jnp.sum(hidden * hidden, axis=1, keepdims=True)
    cross = jnp.sum(hidden * tangent_hidden, axis=1, keepdims=True)
    norm_all[d] = jnp.where(lane < 1, squares, cross)

    def norm_copy(step):
        return pltpu.make_async_remote_copy(
            norm_all.at[d], norm_all.at[d], norm_s.at[step], norm_r.at[step],
            device_id={"dp": along_dp(step)}, device_id_type=MESH)

    for step in range(1, n_dp):
        norm_copy(step).start()
    for step in range(1, n_dp):
        norm_copy(step).wait()
    inverse = 1.0 / model
    means = jnp.sum(norm_all[...], axis=0) * inverse
    scale = lax.rsqrt(means[:, 0:1] + EPSILON)
    normed = gain * hidden * scale
    tangent_normed = gain * scale * (tangent_hidden - hidden * scale * scale * means[:, 1:2])
    msg_all[me] = jnp.concatenate([normed, tangent_normed], axis=0).astype(BF16)

    def to_all(src, dst, send, recv):
        def copy(step):
            _, pd, pv = peer_of(step)
            return pltpu.make_async_remote_copy(
                src(step), dst.at[me], send.at[step], recv.at[step],
                device_id={"dp": pd, "vocab": pv}, device_id_type=MESH)

        return copy

    def start_all(copy):
        @pl.loop(1, n_all)
        def _(step):
            copy(step).start()

    def wait_all(copy):
        @pl.loop(1, n_all)
        def _(step):
            copy(step).wait()

    mate = v + 1 - 2 * lax.rem(v, 2)

    def msg_copy(step):
        _, pd, pv = peer_of(2 * step)
        return pltpu.make_async_remote_copy(
            msg_all.at[me], msg_all.at[me], msg_s.at[step], msg_r.at[step],
            device_id={"dp": pd, "vocab": pv}, device_id_type=MESH)

    def pass_copy(step):
        came_from = lax.rem(me + n_all - 2 * step, n_all)
        return pltpu.make_async_remote_copy(
            msg_all.at[came_from], msg_all.at[came_from], pass_s.at[step], pass_r.at[step],
            device_id={"vocab": mate}, device_id_type=MESH)

    for step in range(1, n_all // 2):
        msg_copy(step).start()
    pass_copy(0).start()
    loads[7].wait()
    for step in range(1, n_all // 2):
        msg_copy(step).wait_recv()
        pass_copy(step).start()
    for step in range(1, n_all // 2):
        msg_copy(step).wait_send()
    for step in range(n_all // 2):
        pass_copy(step).wait()

    pair = jnp.zeros((n_vocab * 2 * ROWS, columns), F32)
    for block in range(n_dp):
        pair = pair + jnp.dot(
            msg_all[block * n_vocab : (block + 1) * n_vocab].reshape(n_vocab * 2 * ROWS, wide),
            head[block * wide : (block + 1) * wide, :],
            preferred_element_type=F32,
        )
    pair = pair.reshape(n_vocab, 2 * ROWS, columns)
    logits = pair[:, 0:ROWS].reshape(live, columns)
    squashed = jnp.tanh(logits * (1.0 / SOFT_CAP))
    slopes = 1.0 - squashed * squashed
    tangent_capped = slopes * pair[:, ROWS:].reshape(live, columns)
    exp_values = jnp.exp(SOFT_CAP * squashed)
    column_at = lax.broadcasted_iota(jnp.int32, (live, columns), 1) + me * columns
    total = jnp.sum(exp_values, axis=1, keepdims=True)
    weighted = jnp.sum(exp_values * tangent_capped, axis=1, keepdims=True)
    picked = jnp.sum(jnp.where(column_at == wanted, tangent_capped, 0.0), axis=1, keepdims=True)
    stat_lane = lax.broadcasted_iota(jnp.int32, (live, LANES), 1)
    stats = (
        jnp.where(stat_lane == 0, total, 0.0)
        + jnp.where(stat_lane == 1, weighted, 0.0)
        + jnp.where(stat_lane == 2, picked, 0.0)
    )
    if live < LANES:
        stats = jnp.concatenate([stats, jnp.zeros((LANES - live, LANES), F32)], axis=0)
    stat_all[me] = stats.T[0:ROWS]
    stat_copy = to_all(lambda step: stat_all.at[me], stat_all, stat_s, stat_r)
    start_all(stat_copy)
    wait_all(stat_copy)
    across = jnp.sum(stat_all[...], axis=0)
    across = jnp.concatenate([across, jnp.zeros((LANES - ROWS, LANES), F32)], axis=0).T[0:live]
    all_total = across[:, 0:1]
    tangent_mean = across[:, 1:2] / all_total
    token = across[:, 2:3] - tangent_mean
    token_row = lax.broadcasted_iota(jnp.int32, (live, slots // 2), 0)
    token_lane = lax.broadcasted_iota(jnp.int32, (live, slots // 2), 1) + d * (slots // 2)
    token_ref[...] = jnp.sum(jnp.where(token_row == token_lane, token, 0.0), axis=0, keepdims=True)

    back_logits = (exp_values / all_total * (tangent_capped - tangent_mean) * slopes).astype(BF16)
    inner_part = jnp.sum(back_logits.astype(F32) * logits, axis=1, keepdims=True)
    high = inner_part.astype(BF16).astype(F32)
    middle = (inner_part - high).astype(BF16).astype(F32)
    low = inner_part - high - middle
    inner_tail = (
        jnp.where(stat_lane == 0, high, 0.0)
        + jnp.where(stat_lane == 1, middle, 0.0)
        + jnp.where(stat_lane == 2, low, 0.0)
    ).reshape(n_vocab, ROWS, LANES)
    for block in range(n_dp):
        part = lax.dot_general(
            back_logits, head[block * wide : (block + 1) * wide, :], NT, preferred_element_type=F32
        ).reshape(n_vocab, ROWS, wide)
        part_send[block * n_vocab : (block + 1) * n_vocab, :, 0:wide] = part.astype(BF16)
        part_send[block * n_vocab : (block + 1) * n_vocab, :, base:] = inner_tail.astype(BF16)

    def part_src(step):
        peer, _, _ = peer_of(step)
        return part_send.at[peer]

    part_copy = to_all(part_src, part_all, part_s, part_r)
    start_all(part_copy)
    part_all[me] = part_send[me]
    wait_all(part_copy)
    back_gain = gain * jnp.sum(part_all[:, :, 0:wide].astype(F32), axis=0)
    inner_back = jnp.sum(jnp.sum(part_all[:, :, base:].astype(F32), axis=0), axis=1, keepdims=True) * inverse
    bh_all[v] = (scale * back_gain - hidden * (scale * scale * inner_back)).astype(BF16)

    def bh_copy(step):
        return pltpu.make_async_remote_copy(
            bh_all.at[v], bh_all.at[v], bh_s.at[step], bh_r.at[step],
            device_id={"vocab": along_vocab(step)}, device_id_type=MESH)

    for step in range(1, n_vocab):
        bh_copy(step).start()
    for step in range(1, n_vocab):
        bh_copy(step).wait()
    back_ref[...] = bh_all[...].astype(F32).reshape(live, wide).astype(BF16)


def local(n_dp, n_vocab, tokens_in, attention, out_projection, tangent, norm_gain, head_weight, lengths, sampled):
    slots, model = tokens_in.shape
    features, wide = out_projection.shape
    columns = head_weight.shape[1]
    live_dev = slots // 2
    live = live_dev * n_dp
    assert live == n_vocab * ROWS and live <= LANES
    n_all = n_dp * n_vocab
    padded = -(-wide // LANES) * LANES + LANES
    vmem, hbm = pl.BlockSpec(memory_space=pltpu.VMEM), pl.BlockSpec(memory_space=pltpu.HBM)
    dma = pltpu.SemaphoreType.DMA
    packed, back, token_mine = pl.pallas_call(
        functools.partial(fused_kernel, n_dp, n_vocab),
        out_shape=(
            jax.ShapeDtypeStruct((live, features), BF16),
            jax.ShapeDtypeStruct((live, wide), BF16),
            jax.ShapeDtypeStruct((1, live_dev), F32),
        ),
        in_specs=[hbm] * 8,
        out_specs=(vmem, vmem, vmem),
        scratch_shapes=[
            pltpu.SMEM(lengths.shape, jnp.int32),
            pltpu.VMEM((1, n_dp * slots), jnp.int32),
            pltpu.VMEM((1, model), BF16),
            pltpu.VMEM((slots, model), BF16),
            pltpu.VMEM((n_dp, slots, wide), BF16),
            pltpu.VMEM((n_dp, slots, wide), BF16),
            pltpu.VMEM((n_dp, slots, features), BF16),
            pltpu.VMEM((features, wide), BF16),
            pltpu.VMEM((features, wide), F32),
            pltpu.VMEM((features, wide), BF16),
            pltpu.VMEM((model, columns), BF16),
            pltpu.VMEM((n_vocab, ROWS, wide), F32),
            pltpu.VMEM((n_vocab, ROWS, wide), F32),
            pltpu.VMEM((n_vocab, ROWS, wide), F32),
            pltpu.VMEM((n_vocab, ROWS, wide), F32),
            pltpu.VMEM((n_dp, ROWS, LANES), F32),
            pltpu.VMEM((n_all, 2 * ROWS, wide), BF16),
            pltpu.VMEM((n_all, ROWS, LANES), F32),
            pltpu.VMEM((n_all, ROWS, padded), BF16),
            pltpu.VMEM((n_all, ROWS, padded), BF16),
            pltpu.VMEM((n_vocab, ROWS, wide), BF16),
            dma((8,)),
            dma((n_dp,)), dma((n_dp,)), dma((n_dp,)), dma((n_dp,)),
            dma((n_vocab,)), dma((n_vocab,)), dma((n_vocab,)), dma((n_vocab,)),
            dma((n_dp,)), dma((n_dp,)),
            dma((n_all // 2,)), dma((n_all // 2,)), dma((n_all // 2,)), dma((n_all // 2,)), dma((n_all,)), dma((n_all,)), dma((n_all,)), dma((n_all,)),
            dma((n_vocab,)), dma((n_vocab,)),
        ],
        compiler_params=pltpu.CompilerParams(
            collective_id=0, has_side_effects=True, vmem_limit_bytes=63 * 1024 * 1024
        ),
    )(lengths, sampled.reshape(1, -1), norm_gain.reshape(1, -1),
      tokens_in, attention, out_projection, tangent, head_weight)
    fisher_product = lax.dot_general(packed, back, (((0,), (0,)), ((), ())), preferred_element_type=F32)
    return (fisher_product, token_mine.reshape(-1))


def solution(mesh):
    return jax.shard_map(
        functools.partial(local, mesh.shape["dp"], mesh.shape["vocab"]),
        mesh=mesh,
        in_specs=(
            P(("groups", "dp"), None),
            P(("groups", "dp"), "vocab"),
            P("vocab", "dp"),
            P(("groups", "vocab"), "dp"),
            P(),
            P(None, ("dp", "vocab")),
            P("groups"),
            P("groups"),
        ),
        out_specs=(P(("groups", "vocab"), "dp"), P(("groups", "dp"))),
        check_vma=False,
    )
```

```python
import functools

import jax
import jax.numpy as jnp
from jax import lax
from jax.experimental import pallas as pl
from jax.experimental.pallas import tpu as pltpu
from jax.sharding import PartitionSpec as P

SOFT_CAP = 30.0
EPSILON = 1e-06
MESH = pl.DeviceIdType.MESH
LANES = 128
ROWS = 8
F32 = jnp.float32
BF16 = jnp.bfloat16
NT = (((1,), (1,)), ((), ()))


def fused_kernel(
    n_dp, n_vocab,
    lengths_hbm, sampled_hbm, gain_hbm, tokens_hbm, attention_hbm, projection_hbm, tangent_hbm, head_hbm,
    packed_ref, back_ref, token_ref,
    lengths_ref, sampled_ref, gain_ref, tokens_own, tokens_send, tokens_all, attention_all, projection, tangent, tangent_narrow, head,
    hid_send, hid_all, tan_send, tan_all, norm_all, msg_all, stat_all, part_send, part_all, bh_all,
    local_sem, att_s, att_r, tok_s, tok_r, hid_s, hid_r, tan_s, tan_r, norm_s, norm_r,
    msg_s, msg_r, pass_s, pass_r, stat_s, stat_r, part_s, part_r, bh_s, bh_r,
):
    d, v = lax.axis_index("dp"), lax.axis_index("vocab")
    n_all = n_dp * n_vocab
    me = d * n_vocab + v
    slots = tokens_all.shape[1]
    wide = tokens_all.shape[2]
    live = n_vocab * ROWS
    model = wide * n_dp
    columns = head.shape[1]
    base = part_all.shape[2] - LANES

    loads = [
        pltpu.make_async_copy(attention_hbm, attention_all.at[d], local_sem.at[0]),
        pltpu.make_async_copy(tokens_hbm, tokens_own, local_sem.at[1]),
        pltpu.make_async_copy(projection_hbm, projection, local_sem.at[2]),
        pltpu.make_async_copy(tangent_hbm, tangent, local_sem.at[3]),
        pltpu.make_async_copy(lengths_hbm, lengths_ref, local_sem.at[5]),
        pltpu.make_async_copy(sampled_hbm, sampled_ref, local_sem.at[6]),
        pltpu.make_async_copy(gain_hbm, gain_ref, local_sem.at[7]),
        pltpu.make_async_copy(head_hbm, head, local_sem.at[4]),
    ]
    for load in loads:
        load.start()

    def peer_of(step):
        peer = lax.rem(me + step, n_all)
        return peer, lax.div(peer, n_vocab), lax.rem(peer, n_vocab)

    def along_dp(step):
        return lax.rem(d + step, n_dp)

    def along_vocab(step):
        return lax.rem(v + step, n_vocab)

    barrier = pltpu.get_barrier_semaphore()
    for step in range(1, n_dp):
        pl.semaphore_signal(barrier, inc=1, device_id={"dp": along_dp(step)}, device_id_type=MESH)
    for step in range(1, n_vocab):
        pl.semaphore_signal(barrier, inc=1, device_id={"vocab": along_vocab(step)}, device_id_type=MESH)
    pl.semaphore_wait(barrier, n_dp + n_vocab - 2)

    def att_copy(step):
        return pltpu.make_async_remote_copy(
            attention_hbm, attention_all.at[d], att_s.at[step], att_r.at[step],
            device_id={"dp": along_dp(step)}, device_id_type=MESH)

    def tok_copy(step):
        return pltpu.make_async_remote_copy(
            tokens_send.at[along_dp(step)], tokens_all.at[d], tok_s.at[step], tok_r.at[step],
            device_id={"dp": along_dp(step)}, device_id_type=MESH)

    for step in range(1, n_dp):
        att_copy(step).start()
    loads[1].wait()
    for block in range(n_dp):
        tokens_send[block] = tokens_own[:, block * wide : (block + 1) * wide]
    tokens_all[d] = tokens_send[d]

    for load in loads[4:7]:
        load.wait()

    slot_at = lax.broadcasted_iota(jnp.int32, (live, n_dp * slots), 1)
    row_at = lax.broadcasted_iota(jnp.int32, (live, n_dp * slots), 0)
    hit = jnp.zeros((live, n_dp * slots), jnp.bool_)
    start = jnp.int32(0)
    for block in range(n_dp):
        length = lengths_ref[block]
        place = slot_at - block * slots
        hit = hit | ((place >= 0) & (place < length) & (row_at == start + place))
        start = start + length
    pick = jnp.where(hit, 1.0, 0.0)
    pick_narrow = pick.astype(BF16)
    wanted = jnp.sum(pick * sampled_ref[...].astype(F32), axis=1, keepdims=True).astype(jnp.int32)

    gain = jnp.zeros((1, wide), F32)
    for block in range(n_dp):
        gain = jnp.where(d == block, gain_ref[:, block * wide : (block + 1) * wide].astype(F32), gain)

    loads[3].wait()
    tangent_narrow[...] = tangent[...].astype(BF16)
    loads[2].wait()
    loads[0].wait()
    for step in range(1, n_dp):
        att_copy(step).wait()
    for step in range(1, n_dp):
        tok_copy(step).start()
    everything = attention_all[...].reshape(n_dp * slots, attention_all.shape[2])
    packed = jnp.dot(pick_narrow, everything, preferred_element_type=F32).astype(BF16)
    packed_ref[...] = packed

    def chunk_copy(src, dst, send, recv):
        def copy(step):
            return pltpu.make_async_remote_copy(
                src.at[along_vocab(step)], dst.at[v], send.at[step], recv.at[step],
                device_id={"vocab": along_vocab(step)}, device_id_type=MESH)

        return copy

    hid_copy = chunk_copy(hid_send, hid_all, hid_s, hid_r)
    tan_copy = chunk_copy(tan_send, tan_all, tan_s, tan_r)
    hid_send[...] = jnp.dot(packed, projection[...], preferred_element_type=F32).reshape(n_vocab, ROWS, wide)
    for step in range(1, n_vocab):
        hid_copy(step).start()
    hid_all[v] = hid_send[v]
    tan_send[...] = jnp.dot(packed, tangent_narrow[...], preferred_element_type=F32).reshape(n_vocab, ROWS, wide)
    for step in range(1, n_vocab):
        tan_copy(step).start()
    tan_all[v] = tan_send[v]

    for step in range(1, n_dp):
        tok_copy(step).wait()
    my_slot = lax.broadcasted_iota(jnp.int32, (ROWS, live), 1)
    my_row = lax.broadcasted_iota(jnp.int32, (ROWS, live), 0) + v * ROWS
    own_rows = jnp.where(my_slot == my_row, 1.0, 0.0)
    own_pick = jnp.dot(own_rows.astype(BF16), pick_narrow, preferred_element_type=F32).astype(BF16)
    tokens = jnp.dot(
        own_pick, tokens_all[...].reshape(n_dp * slots, wide), preferred_element_type=F32
    )
    for step in range(1, n_vocab):
        hid_copy(step).wait()
    hidden = tokens + jnp.sum(hid_all[...], axis=0)
    for step in range(1, n_vocab):
        tan_copy(step).wait()
    tangent_hidden = jnp.sum(tan_all[...], axis=0)

    lane = lax.broadcasted_iota(jnp.int32, (ROWS, LANES), 1)
    squares = jnp.sum(hidden * hidden, axis=1, keepdims=True)
    cross = jnp.sum(hidden * tangent_hidden, axis=1, keepdims=True)
    norm_all[d] = jnp.where(lane < 1, squares, cross)

    def norm_copy(step):
        return pltpu.make_async_remote_copy(
            norm_all.at[d], norm_all.at[d], norm_s.at[step], norm_r.at[step],
            device_id={"dp": along_dp(step)}, device_id_type=MESH)

    for step in range(1, n_dp):
        norm_copy(step).start()
    for step in range(1, n_dp):
        norm_copy(step).wait()
    inverse = 1.0 / model
    means = jnp.sum(norm_all[...], axis=0) * inverse
    scale = lax.rsqrt(means[:, 0:1] + EPSILON)
    normed = gain * hidden * scale
    tangent_normed = gain * scale * (tangent_hidden - hidden * scale * scale * means[:, 1:2])
    msg_all[me] = jnp.concatenate([normed, tangent_normed], axis=0).astype(BF16)

    def to_all(src, dst, send, recv):
        def copy(step):
            _, pd, pv = peer_of(step)
            return pltpu.make_async_remote_copy(
                src(step), dst.at[me], send.at[step], recv.at[step],
                device_id={"dp": pd, "vocab": pv}, device_id_type=MESH)

        return copy

    def start_all(copy):
        if n_all <= 16:
            for step in range(1, n_all):
                copy(step).start()
        else:

            @pl.loop(1, n_all)
            def _(step):
                copy(step).start()

    def wait_all(copy):
        if n_all <= 16:
            for step in range(1, n_all):
                copy(step).wait()
        else:

            @pl.loop(1, n_all)
            def _(step):
                copy(step).wait()

    mate = v + 1 - 2 * lax.rem(v, 2)

    half = n_vocab // 2

    def msg_copy(far, step):
        slot = far * half + step
        return pltpu.make_async_remote_copy(
            msg_all.at[me], msg_all.at[me], msg_s.at[slot], msg_r.at[slot],
            device_id={"dp": along_dp(far), "vocab": along_vocab(2 * step)}, device_id_type=MESH)

    def pass_copy(far, step):
        slot = far * half + step
        came_from = along_dp(n_dp - far) * n_vocab + along_vocab(n_vocab - 2 * step)
        return pltpu.make_async_remote_copy(
            msg_all.at[came_from], msg_all.at[came_from], pass_s.at[slot], pass_r.at[slot],
            device_id={"vocab": mate}, device_id_type=MESH)

    hops = [(far, step) for far in range(n_dp) for step in range(half) if far + step > 0]
    for far, step in hops:
        msg_copy(far, step).start()
    pair = jnp.zeros((n_vocab * 2 * ROWS, columns), F32)
    for far in range(n_dp + 1):
        if far < n_dp:
            for step in range(half):
                if far + step > 0:
                    msg_copy(far, step).wait_recv()
                pass_copy(far, step).start()
        if far == 0:
            loads[7].wait()
            continue
        for step in range(half):
            pass_copy(far - 1, step).wait()
        block = along_dp(n_dp - far + 1)
        pair = pair + jnp.dot(
            msg_all[pl.ds(block * n_vocab, n_vocab)].reshape(n_vocab * 2 * ROWS, wide),
            head[pl.ds(pl.multiple_of(block * wide, 32), wide), :],
            preferred_element_type=F32,
        )
    for far, step in hops:
        msg_copy(far, step).wait_send()
    pair = pair.reshape(n_vocab, 2 * ROWS, columns)
    logits = pair[:, 0:ROWS].reshape(live, columns)
    squashed = jnp.tanh(logits * (1.0 / SOFT_CAP))
    slopes = 1.0 - squashed * squashed
    tangent_capped = slopes * pair[:, ROWS:].reshape(live, columns)
    exp_values = jnp.exp(SOFT_CAP * squashed)
    column_at = lax.broadcasted_iota(jnp.int32, (live, columns), 1) + me * columns
    total = jnp.sum(exp_values, axis=1, keepdims=True)
    weighted = jnp.sum(exp_values * tangent_capped, axis=1, keepdims=True)
    picked = jnp.sum(jnp.where(column_at == wanted, tangent_capped, 0.0), axis=1, keepdims=True)
    stat_lane = lax.broadcasted_iota(jnp.int32, (live, LANES), 1)
    stats = (
        jnp.where(stat_lane == 0, total, 0.0)
        + jnp.where(stat_lane == 1, weighted, 0.0)
        + jnp.where(stat_lane == 2, picked, 0.0)
    )
    if live < LANES:
        stats = jnp.concatenate([stats, jnp.zeros((LANES - live, LANES), F32)], axis=0)
    stat_all[me] = stats.T[0:ROWS]
    stat_copy = to_all(lambda step: stat_all.at[me], stat_all, stat_s, stat_r)
    start_all(stat_copy)
    wait_all(stat_copy)
    across = jnp.sum(stat_all[...], axis=0)
    across = jnp.concatenate([across, jnp.zeros((LANES - ROWS, LANES), F32)], axis=0).T[0:live]
    all_total = across[:, 0:1]
    tangent_mean = across[:, 1:2] / all_total
    token = across[:, 2:3] - tangent_mean
    token_row = lax.broadcasted_iota(jnp.int32, (live, slots // 2), 0)
    token_lane = lax.broadcasted_iota(jnp.int32, (live, slots // 2), 1) + d * (slots // 2)
    token_ref[...] = jnp.sum(jnp.where(token_row == token_lane, token, 0.0), axis=0, keepdims=True)

    back_logits = (exp_values / all_total * (tangent_capped - tangent_mean) * slopes).astype(BF16)
    inner_part = jnp.sum(back_logits.astype(F32) * logits, axis=1, keepdims=True)
    high = inner_part.astype(BF16).astype(F32)
    middle = (inner_part - high).astype(BF16).astype(F32)
    low = inner_part - high - middle
    inner_tail = (
        jnp.where(stat_lane == 0, high, 0.0)
        + jnp.where(stat_lane == 1, middle, 0.0)
        + jnp.where(stat_lane == 2, low, 0.0)
    ).reshape(n_vocab, ROWS, LANES)
    def part_copy(far, step):
        slot = far * n_vocab + step
        peer_v = along_vocab(step)
        return pltpu.make_async_remote_copy(
            part_send.at[along_dp(far) * n_vocab + peer_v], part_all.at[me], part_s.at[slot], part_r.at[slot],
            device_id={"dp": along_dp(far), "vocab": peer_v}, device_id_type=MESH)

    for far in [*range(1, n_dp), 0]:
        block = along_dp(far)
        part = lax.dot_general(
            back_logits,
            head[pl.ds(pl.multiple_of(block * wide, 32), wide), :],
            NT,
            preferred_element_type=F32,
        ).reshape(n_vocab, ROWS, wide)
        part_send[pl.ds(block * n_vocab, n_vocab), :, 0:wide] = part.astype(BF16)
        part_send[pl.ds(block * n_vocab, n_vocab), :, base:] = inner_tail.astype(BF16)
        for step in range(n_vocab):
            if far + step > 0:
                part_copy(far, step).start()
    part_all[me] = part_send[me]
    for far in range(n_dp):
        for step in range(n_vocab):
            if far + step > 0:
                part_copy(far, step).wait()
    back_gain = gain * jnp.sum(part_all[:, :, 0:wide].astype(F32), axis=0)
    inner_back = jnp.sum(jnp.sum(part_all[:, :, base:].astype(F32), axis=0), axis=1, keepdims=True) * inverse
    bh_all[v] = (scale * back_gain - hidden * (scale * scale * inner_back)).astype(BF16)

    def bh_copy(step):
        return pltpu.make_async_remote_copy(
            bh_all.at[v], bh_all.at[v], bh_s.at[step], bh_r.at[step],
            device_id={"vocab": along_vocab(step)}, device_id_type=MESH)

    for step in range(1, n_vocab):
        bh_copy(step).start()
    for step in range(1, n_vocab):
        bh_copy(step).wait()
    back_ref[...] = bh_all[...].astype(F32).reshape(live, wide).astype(BF16)


def local(n_dp, n_vocab, tokens_in, attention, out_projection, tangent, norm_gain, head_weight, lengths, sampled):
    slots, model = tokens_in.shape
    features, wide = out_projection.shape
    columns = head_weight.shape[1]
    live_dev = slots // 2
    live = live_dev * n_dp
    assert live == n_vocab * ROWS and live <= LANES
    n_all = n_dp * n_vocab
    padded = -(-wide // LANES) * LANES + LANES
    vmem, hbm = pl.BlockSpec(memory_space=pltpu.VMEM), pl.BlockSpec(memory_space=pltpu.HBM)
    dma = pltpu.SemaphoreType.DMA
    packed, back, token_mine = pl.pallas_call(
        functools.partial(fused_kernel, n_dp, n_vocab),
        out_shape=(
            jax.ShapeDtypeStruct((live, features), BF16),
            jax.ShapeDtypeStruct((live, wide), BF16),
            jax.ShapeDtypeStruct((1, live_dev), F32),
        ),
        in_specs=[hbm] * 8,
        out_specs=(vmem, vmem, vmem),
        scratch_shapes=[
            pltpu.SMEM(lengths.shape, jnp.int32),
            pltpu.VMEM((1, n_dp * slots), jnp.int32),
            pltpu.VMEM((1, model), BF16),
            pltpu.VMEM((slots, model), BF16),
            pltpu.VMEM((n_dp, slots, wide), BF16),
            pltpu.VMEM((n_dp, slots, wide), BF16),
            pltpu.VMEM((n_dp, slots, features), BF16),
            pltpu.VMEM((features, wide), BF16),
            pltpu.VMEM((features, wide), F32),
            pltpu.VMEM((features, wide), BF16),
            pltpu.VMEM((model, columns), BF16),
            pltpu.VMEM((n_vocab, ROWS, wide), F32),
            pltpu.VMEM((n_vocab, ROWS, wide), F32),
            pltpu.VMEM((n_vocab, ROWS, wide), F32),
            pltpu.VMEM((n_vocab, ROWS, wide), F32),
            pltpu.VMEM((n_dp, ROWS, LANES), F32),
            pltpu.VMEM((n_all, 2 * ROWS, wide), BF16),
            pltpu.VMEM((n_all, ROWS, LANES), F32),
            pltpu.VMEM((n_all, ROWS, padded), BF16),
            pltpu.VMEM((n_all, ROWS, padded), BF16),
            pltpu.VMEM((n_vocab, ROWS, wide), BF16),
            dma((8,)),
            dma((n_dp,)), dma((n_dp,)), dma((n_dp,)), dma((n_dp,)),
            dma((n_vocab,)), dma((n_vocab,)), dma((n_vocab,)), dma((n_vocab,)),
            dma((n_dp,)), dma((n_dp,)),
            dma((n_all // 2,)), dma((n_all // 2,)), dma((n_all // 2,)), dma((n_all // 2,)), dma((n_all,)), dma((n_all,)), dma((n_all,)), dma((n_all,)),
            dma((n_vocab,)), dma((n_vocab,)),
        ],
        compiler_params=pltpu.CompilerParams(
            collective_id=0, has_side_effects=True, vmem_limit_bytes=63 * 1024 * 1024
        ),
    )(lengths, sampled.reshape(1, -1), norm_gain.reshape(1, -1),
      tokens_in, attention, out_projection, tangent, head_weight)
    fisher_product = lax.dot_general(packed, back, (((0,), (0,)), ((), ())), preferred_element_type=F32)
    return (fisher_product, token_mine.reshape(-1))


def solution(mesh):
    return jax.shard_map(
        functools.partial(local, mesh.shape["dp"], mesh.shape["vocab"]),
        mesh=mesh,
        in_specs=(
            P(("groups", "dp"), None),
            P(("groups", "dp"), "vocab"),
            P("vocab", "dp"),
            P(("groups", "vocab"), "dp"),
            P(),
            P(None, ("dp", "vocab")),
            P("groups"),
            P("groups"),
        ),
        out_specs=(P(("groups", "vocab"), "dp"), P(("groups", "dp"))),
        check_vma=False,
    )
```

```python
import functools

import jax
import jax.numpy as jnp
from jax import lax
from jax.experimental import pallas as pl
from jax.experimental.pallas import tpu as pltpu
from jax.sharding import PartitionSpec as P

SOFT_CAP = 30.0
EPSILON = 1e-06
MESH = pl.DeviceIdType.MESH
LANES = 128
ROWS = 8
F32 = jnp.float32
BF16 = jnp.bfloat16
NT = (((1,), (1,)), ((), ()))


def fused_kernel(
    n_dp, n_vocab,
    lengths_hbm, sampled_hbm, gain_hbm, tokens_hbm, attention_hbm, projection_hbm, tangent_hbm, head_hbm,
    packed_ref, back_ref, token_ref,
    lengths_ref, sampled_ref, gain_ref, tokens_own, tokens_send, tokens_all, attention_all, projection, tangent, tangent_narrow, head,
    hid_send, hid_all, tan_send, tan_all, norm_all, msg_all, stat_all, pair_send, pair_got, part_send, part_all, bh_all,
    local_sem, att_s, att_r, tok_s, tok_r, hid_s, hid_r, tan_s, tan_r, norm_s, norm_r,
    msg_s, msg_r, pass_s, pass_r, stat_s, stat_r, pair_s, pair_r, part_s, part_r, bh_s, bh_r,
):
    d, v = lax.axis_index("dp"), lax.axis_index("vocab")
    n_all = n_dp * n_vocab
    me = d * n_vocab + v
    slots = tokens_all.shape[1]
    wide = tokens_all.shape[2]
    live = n_vocab * ROWS
    model = wide * n_dp
    columns = head.shape[1]
    base = part_all.shape[2] - LANES

    loads = [
        pltpu.make_async_copy(attention_hbm, attention_all.at[d], local_sem.at[0]),
        pltpu.make_async_copy(tokens_hbm, tokens_own, local_sem.at[1]),
        pltpu.make_async_copy(projection_hbm, projection, local_sem.at[2]),
        pltpu.make_async_copy(tangent_hbm, tangent, local_sem.at[3]),
        pltpu.make_async_copy(lengths_hbm, lengths_ref, local_sem.at[5]),
        pltpu.make_async_copy(sampled_hbm, sampled_ref, local_sem.at[6]),
        pltpu.make_async_copy(gain_hbm, gain_ref, local_sem.at[7]),
        pltpu.make_async_copy(head_hbm, head, local_sem.at[4]),
    ]
    for load in loads:
        load.start()

    def peer_of(step):
        peer = lax.rem(me + step, n_all)
        return peer, lax.div(peer, n_vocab), lax.rem(peer, n_vocab)

    def along_dp(step):
        return lax.rem(d + step, n_dp)

    def along_vocab(step):
        return lax.rem(v + step, n_vocab)

    barrier = pltpu.get_barrier_semaphore()
    for step in range(1, n_dp):
        pl.semaphore_signal(barrier, inc=1, device_id={"dp": along_dp(step)}, device_id_type=MESH)
    for step in range(1, n_vocab):
        pl.semaphore_signal(barrier, inc=1, device_id={"vocab": along_vocab(step)}, device_id_type=MESH)
    pl.semaphore_wait(barrier, n_dp + n_vocab - 2)

    def att_copy(step):
        return pltpu.make_async_remote_copy(
            attention_hbm, attention_all.at[d], att_s.at[step], att_r.at[step],
            device_id={"dp": along_dp(step)}, device_id_type=MESH)

    def tok_copy(step):
        return pltpu.make_async_remote_copy(
            tokens_send.at[along_dp(step)], tokens_all.at[d], tok_s.at[step], tok_r.at[step],
            device_id={"dp": along_dp(step)}, device_id_type=MESH)

    for step in range(1, n_dp):
        att_copy(step).start()
    loads[1].wait()
    for block in range(n_dp):
        tokens_send[block] = tokens_own[:, block * wide : (block + 1) * wide]
    tokens_all[d] = tokens_send[d]

    for load in loads[4:7]:
        load.wait()

    slot_at = lax.broadcasted_iota(jnp.int32, (live, n_dp * slots), 1)
    row_at = lax.broadcasted_iota(jnp.int32, (live, n_dp * slots), 0)
    hit = jnp.zeros((live, n_dp * slots), jnp.bool_)
    start = jnp.int32(0)
    for block in range(n_dp):
        length = lengths_ref[block]
        place = slot_at - block * slots
        hit = hit | ((place >= 0) & (place < length) & (row_at == start + place))
        start = start + length
    pick = jnp.where(hit, 1.0, 0.0)
    pick_narrow = pick.astype(BF16)
    wanted = jnp.sum(pick * sampled_ref[...].astype(F32), axis=1, keepdims=True).astype(jnp.int32)

    gain_row = gain_ref[...].astype(F32).reshape(1, model)
    gain = jnp.zeros((1, wide), F32)
    for block in range(n_dp):
        gain = jnp.where(d == block, gain_row[:, block * wide : (block + 1) * wide], gain)

    loads[3].wait()
    tangent_narrow[...] = tangent[...].astype(BF16)
    loads[2].wait()
    loads[0].wait()
    for step in range(1, n_dp):
        att_copy(step).wait()
    for step in range(1, n_dp):
        tok_copy(step).start()
    everything = attention_all[...].reshape(n_dp * slots, attention_all.shape[2])
    packed = jnp.dot(pick_narrow, everything, preferred_element_type=F32).astype(BF16)
    packed_ref[...] = packed

    def chunk_copy(src, dst, send, recv):
        def copy(step):
            return pltpu.make_async_remote_copy(
                src.at[along_vocab(step)], dst.at[v], send.at[step], recv.at[step],
                device_id={"vocab": along_vocab(step)}, device_id_type=MESH)

        return copy

    hid_copy = chunk_copy(hid_send, hid_all, hid_s, hid_r)
    tan_copy = chunk_copy(tan_send, tan_all, tan_s, tan_r)
    hid_send[...] = jnp.dot(packed, projection[...], preferred_element_type=F32).reshape(n_vocab, ROWS, wide)
    for step in range(1, n_vocab):
        hid_copy(step).start()
    hid_all[v] = hid_send[v]
    tan_send[...] = jnp.dot(packed, tangent_narrow[...], preferred_element_type=F32).reshape(n_vocab, ROWS, wide)
    for step in range(1, n_vocab):
        tan_copy(step).start()
    tan_all[v] = tan_send[v]

    for step in range(1, n_dp):
        tok_copy(step).wait()
    my_slot = lax.broadcasted_iota(jnp.int32, (ROWS, live), 1)
    my_row = lax.broadcasted_iota(jnp.int32, (ROWS, live), 0) + v * ROWS
    own_rows = jnp.where(my_slot == my_row, 1.0, 0.0)
    own_pick = jnp.dot(own_rows.astype(BF16), pick_narrow, preferred_element_type=F32).astype(BF16)
    tokens = jnp.dot(
        own_pick, tokens_all[...].reshape(n_dp * slots, wide), preferred_element_type=F32
    )
    for step in range(1, n_vocab):
        hid_copy(step).wait()
    hidden = tokens + jnp.sum(hid_all[...], axis=0)
    for step in range(1, n_vocab):
        tan_copy(step).wait()
    tangent_hidden = jnp.sum(tan_all[...], axis=0)

    lane = lax.broadcasted_iota(jnp.int32, (ROWS, LANES), 1)
    squares = jnp.sum(hidden * hidden, axis=1, keepdims=True)
    cross = jnp.sum(hidden * tangent_hidden, axis=1, keepdims=True)
    norm_all[d] = jnp.where(lane < 1, squares, cross)

    def norm_copy(step):
        return pltpu.make_async_remote_copy(
            norm_all.at[d], norm_all.at[d], norm_s.at[step], norm_r.at[step],
            device_id={"dp": along_dp(step)}, device_id_type=MESH)

    for step in range(1, n_dp):
        norm_copy(step).start()
    for step in range(1, n_dp):
        norm_copy(step).wait()
    inverse = 1.0 / model
    means = jnp.sum(norm_all[...], axis=0) * inverse
    scale = lax.rsqrt(means[:, 0:1] + EPSILON)
    normed = gain * hidden * scale
    tangent_normed = gain * scale * (tangent_hidden - hidden * scale * scale * means[:, 1:2])
    msg_all[me] = jnp.concatenate([normed, tangent_normed], axis=0).astype(BF16)

    def to_all(src, dst, send, recv):
        def copy(step):
            _, pd, pv = peer_of(step)
            return pltpu.make_async_remote_copy(
                src(step), dst.at[me], send.at[step], recv.at[step],
                device_id={"dp": pd, "vocab": pv}, device_id_type=MESH)

        return copy

    def start_all(copy):
        if n_all <= 16:
            for step in range(1, n_all):
                copy(step).start()
        else:

            @pl.loop(1, n_all)
            def _(step):
                copy(step).start()

    def wait_all(copy):
        if n_all <= 16:
            for step in range(1, n_all):
                copy(step).wait()
        else:

            @pl.loop(1, n_all)
            def _(step):
                copy(step).wait()

    mate = v + 1 - 2 * lax.rem(v, 2)

    half = n_vocab // 2

    def msg_copy(far, step):
        slot = far * half + step
        return pltpu.make_async_remote_copy(
            msg_all.at[me], msg_all.at[me], msg_s.at[slot], msg_r.at[slot],
            device_id={"dp": along_dp(far), "vocab": along_vocab(2 * step)}, device_id_type=MESH)

    def pass_copy(far, step):
        slot = far * half + step
        came_from = along_dp(n_dp - far) * n_vocab + along_vocab(n_vocab - 2 * step)
        return pltpu.make_async_remote_copy(
            msg_all.at[came_from], msg_all.at[came_from], pass_s.at[slot], pass_r.at[slot],
            device_id={"vocab": mate}, device_id_type=MESH)

    hops = [(far, step) for far in range(n_dp) for step in range(half) if far + step > 0]
    for far, step in hops:
        msg_copy(far, step).start()
    pair = jnp.zeros((n_vocab * 2 * ROWS, columns), F32)
    for far in range(n_dp + 1):
        if far < n_dp:
            for step in range(half):
                if far + step > 0:
                    msg_copy(far, step).wait_recv()
                pass_copy(far, step).start()
        if far == 0:
            loads[7].wait()
            continue
        for step in range(half):
            pass_copy(far - 1, step).wait()
        block = along_dp(n_dp - far + 1)
        pair = pair + jnp.dot(
            msg_all[pl.ds(block * n_vocab, n_vocab)].reshape(n_vocab * 2 * ROWS, wide),
            head[pl.ds(pl.multiple_of(block * wide, 32), wide), :],
            preferred_element_type=F32,
        )
    for far, step in hops:
        msg_copy(far, step).wait_send()
    pair = pair.reshape(n_vocab, 2 * ROWS, columns)
    logits = pair[:, 0:ROWS].reshape(live, columns)
    squashed = jnp.tanh(logits * (1.0 / SOFT_CAP))
    slopes = 1.0 - squashed * squashed
    tangent_capped = slopes * pair[:, ROWS:].reshape(live, columns)
    exp_values = jnp.exp(SOFT_CAP * squashed)
    column_at = lax.broadcasted_iota(jnp.int32, (live, columns), 1) + me * columns
    total = jnp.sum(exp_values, axis=1, keepdims=True)
    weighted = jnp.sum(exp_values * tangent_capped, axis=1, keepdims=True)
    picked = jnp.sum(jnp.where(column_at == wanted, tangent_capped, 0.0), axis=1, keepdims=True)
    stat_lane = lax.broadcasted_iota(jnp.int32, (live, LANES), 1)
    stats = (
        jnp.where(stat_lane == 0, total, 0.0)
        + jnp.where(stat_lane == 1, weighted, 0.0)
        + jnp.where(stat_lane == 2, picked, 0.0)
    )
    if live < LANES:
        stats = jnp.concatenate([stats, jnp.zeros((LANES - live, LANES), F32)], axis=0)
    stat_all[me] = stats.T[0:ROWS]
    stat_copy = to_all(lambda step: stat_all.at[me], stat_all, stat_s, stat_r)
    start_all(stat_copy)
    wait_all(stat_copy)
    across = jnp.sum(stat_all[...], axis=0)
    across = jnp.concatenate([across, jnp.zeros((LANES - ROWS, LANES), F32)], axis=0).T[0:live]
    all_total = across[:, 0:1]
    tangent_mean = across[:, 1:2] / all_total
    token = across[:, 2:3] - tangent_mean
    token_row = lax.broadcasted_iota(jnp.int32, (live, slots // 2), 0)
    token_lane = lax.broadcasted_iota(jnp.int32, (live, slots // 2), 1) + d * (slots // 2)
    token_ref[...] = jnp.sum(jnp.where(token_row == token_lane, token, 0.0), axis=0, keepdims=True)

    back_logits = (exp_values / all_total * (tangent_capped - tangent_mean) * slopes).astype(BF16)
    inner_part = jnp.sum(back_logits.astype(F32) * logits, axis=1, keepdims=True)
    inner_tail = jnp.where(stat_lane == 0, inner_part, 0.0).reshape(n_vocab, ROWS, LANES)

    core = lax.rem(v, 2)

    def pair_copy(far, step):
        slot = far * half + step
        return pltpu.make_async_remote_copy(
            pair_send.at[far, 2 * step + 1 - core], pair_got.at[far, step], pair_s.at[slot], pair_r.at[slot],
            device_id={"vocab": mate}, device_id_type=MESH)

    def part_copy(far, step):
        slot = far * half + step
        return pltpu.make_async_remote_copy(
            part_send.at[slot], part_all.at[slot], part_s.at[slot], part_r.at[slot],
            device_id={"dp": along_dp(far), "vocab": along_vocab(2 * step)}, device_id_type=MESH)

    order = [*range(1, n_dp), 0]
    for turn in range(n_dp + 1):
        if turn < n_dp:
            far = order[turn]
            pair_send[far, :, :, 0:wide] = lax.dot_general(
                back_logits,
                head[pl.ds(pl.multiple_of(along_dp(far) * wide, 32), wide), :],
                NT,
                preferred_element_type=F32,
            ).reshape(n_vocab, ROWS, wide)
            pair_send[far, :, :, base:] = inner_tail
            for step in range(half):
                pair_copy(far, step).start()
        if turn == 0:
            continue
        far = order[turn - 1]
        for step in range(half):
            pair_copy(far, step).wait()
        for step in range(half):
            chunk = along_vocab(2 * step)
            got = pair_got[far, lax.div(chunk, 2)]
            added = pair_send[far, chunk, :, 0:wide] + got[:, 0:wide]
            tail = pair_send[far, chunk, :, base:] + got[:, base:]
            tail = tail[:, 0:1]
            high = tail.astype(BF16).astype(F32)
            middle = (tail - high).astype(BF16).astype(F32)
            tail = jnp.where(lane == 0, high, 0.0) + jnp.where(lane == 1, middle, 0.0) + jnp.where(
                lane == 2, tail - high - middle, 0.0
            )
            slot = far * half + step
            target = part_send if slot else part_all
            target[slot, :, 0:wide] = added.astype(BF16)
            target[slot, :, base:] = tail.astype(BF16)
            if slot:
                part_copy(far, step).start()
    for far, step in hops:
        part_copy(far, step).wait()
    back_gain = gain * jnp.sum(part_all[:, :, 0:wide].astype(F32), axis=0)
    inner_back = jnp.sum(jnp.sum(part_all[:, :, base:].astype(F32), axis=0), axis=1, keepdims=True) * inverse
    bh_all[v] = (scale * back_gain - hidden * (scale * scale * inner_back)).astype(BF16)

    def bh_copy(step):
        return pltpu.make_async_remote_copy(
            bh_all.at[v], bh_all.at[v], bh_s.at[step], bh_r.at[step],
            device_id={"vocab": along_vocab(step)}, device_id_type=MESH)

    for step in range(1, n_vocab):
        bh_copy(step).start()
    for step in range(1, n_vocab):
        bh_copy(step).wait()
    back_ref[...] = bh_all[...].astype(F32).reshape(live, wide).astype(BF16)


def local(n_dp, n_vocab, tokens_in, attention, out_projection, tangent, norm_gain, head_weight, lengths, sampled):
    slots, model = tokens_in.shape
    features, wide = out_projection.shape
    columns = head_weight.shape[1]
    live_dev = slots // 2
    live = live_dev * n_dp
    assert live == n_vocab * ROWS and live <= LANES
    n_all = n_dp * n_vocab
    padded = -(-wide // LANES) * LANES + LANES
    vmem, hbm = pl.BlockSpec(memory_space=pltpu.VMEM), pl.BlockSpec(memory_space=pltpu.HBM)
    dma = pltpu.SemaphoreType.DMA
    packed, back, token_mine = pl.pallas_call(
        functools.partial(fused_kernel, n_dp, n_vocab),
        out_shape=(
            jax.ShapeDtypeStruct((live, features), BF16),
            jax.ShapeDtypeStruct((live, wide), BF16),
            jax.ShapeDtypeStruct((1, live_dev), F32),
        ),
        in_specs=[hbm] * 8,
        out_specs=(vmem, vmem, vmem),
        scratch_shapes=[
            pltpu.SMEM(lengths.shape, jnp.int32),
            pltpu.VMEM((1, n_dp * slots), jnp.int32),
            pltpu.VMEM((model,), BF16),
            pltpu.VMEM((slots, model), BF16),
            pltpu.VMEM((n_dp, slots, wide), BF16),
            pltpu.VMEM((n_dp, slots, wide), BF16),
            pltpu.VMEM((n_dp, slots, features), BF16),
            pltpu.VMEM((features, wide), BF16),
            pltpu.VMEM((features, wide), F32),
            pltpu.VMEM((features, wide), BF16),
            pltpu.VMEM((model, columns), BF16),
            pltpu.VMEM((n_vocab, ROWS, wide), F32),
            pltpu.VMEM((n_vocab, ROWS, wide), F32),
            pltpu.VMEM((n_vocab, ROWS, wide), F32),
            pltpu.VMEM((n_vocab, ROWS, wide), F32),
            pltpu.VMEM((n_dp, ROWS, LANES), F32),
            pltpu.VMEM((n_all, 2 * ROWS, wide), BF16),
            pltpu.VMEM((n_all, ROWS, LANES), F32),
            pltpu.VMEM((n_dp, n_vocab, ROWS, padded), F32),
            pltpu.VMEM((n_dp, n_vocab // 2, ROWS, padded), F32),
            pltpu.VMEM((n_all // 2, ROWS, padded), BF16),
            pltpu.VMEM((n_all // 2, ROWS, padded), BF16),
            pltpu.VMEM((n_vocab, ROWS, wide), BF16),
            dma((8,)),
            dma((n_dp,)), dma((n_dp,)), dma((n_dp,)), dma((n_dp,)),
            dma((n_vocab,)), dma((n_vocab,)), dma((n_vocab,)), dma((n_vocab,)),
            dma((n_dp,)), dma((n_dp,)),
            dma((n_all // 2,)), dma((n_all // 2,)), dma((n_all // 2,)), dma((n_all // 2,)),
            dma((n_all,)), dma((n_all,)),
            dma((n_all // 2,)), dma((n_all // 2,)), dma((n_all // 2,)), dma((n_all // 2,)),
            dma((n_vocab,)), dma((n_vocab,)),
        ],
        compiler_params=pltpu.CompilerParams(
            collective_id=0, has_side_effects=True, vmem_limit_bytes=63 * 1024 * 1024
        ),
    )(lengths, sampled.reshape(1, -1), norm_gain,
      tokens_in, attention, out_projection, tangent, head_weight)
    fisher_product = lax.dot_general(packed, back, (((0,), (0,)), ((), ())), preferred_element_type=F32)
    return (fisher_product, token_mine.reshape(-1))


def solution(mesh):
    return jax.shard_map(
        functools.partial(local, mesh.shape["dp"], mesh.shape["vocab"]),
        mesh=mesh,
        in_specs=(
            P(("groups", "dp"), None),
            P(("groups", "dp"), "vocab"),
            P("vocab", "dp"),
            P(("groups", "vocab"), "dp"),
            P(),
            P(None, ("dp", "vocab")),
            P("groups"),
            P("groups"),
        ),
        out_specs=(P(("groups", "vocab"), "dp"), P(("groups", "dp"))),
        check_vma=False,
    )
```

```python
import functools

import jax
import jax.numpy as jnp
from jax import lax
from jax.experimental import pallas as pl
from jax.experimental.pallas import tpu as pltpu
from jax.sharding import PartitionSpec as P

SOFT_CAP = 30.0
EPSILON = 1e-06
MESH = pl.DeviceIdType.MESH
LANES = 128
ROWS = 8
F32 = jnp.float32
BF16 = jnp.bfloat16
NT = (((1,), (1,)), ((), ()))


def fused_kernel(
    n_dp, n_vocab,
    lengths_hbm, sampled_hbm, gain_hbm, tokens_hbm, attention_hbm, projection_hbm, tangent_hbm, head_hbm,
    packed_ref, back_ref, token_ref,
    lengths_ref, sampled_ref, gain_ref, tokens_own, tokens_send, tokens_all, attention_all, projection, tangent, tangent_narrow, head,
    hid_send, hid_all, tan_send, tan_all, norm_all, msg_all, stat_all, pair_send, pair_got, part_send, part_all, bh_all,
    local_sem, att_s, att_r, tok_s, tok_r, hid_s, hid_r, tan_s, tan_r, norm_s, norm_r,
    msg_s, msg_r, pass_s, pass_r, stat_s, stat_r, pair_s, pair_r, part_s, part_r, bh_s, bh_r,
):
    d, v = lax.axis_index("dp"), lax.axis_index("vocab")
    n_all = n_dp * n_vocab
    me = d * n_vocab + v
    slots = tokens_all.shape[1]
    wide = tokens_all.shape[2]
    live = n_vocab * ROWS
    model = wide * n_dp
    columns = head.shape[1]
    base = part_all.shape[2] - LANES

    loads = [
        pltpu.make_async_copy(attention_hbm, attention_all.at[d], local_sem.at[0]),
        pltpu.make_async_copy(tokens_hbm, tokens_own, local_sem.at[1]),
        pltpu.make_async_copy(projection_hbm, projection, local_sem.at[2]),
        pltpu.make_async_copy(tangent_hbm, tangent, local_sem.at[3]),
        pltpu.make_async_copy(lengths_hbm, lengths_ref, local_sem.at[5]),
        pltpu.make_async_copy(sampled_hbm, sampled_ref, local_sem.at[6]),
        pltpu.make_async_copy(gain_hbm, gain_ref, local_sem.at[7]),
        pltpu.make_async_copy(head_hbm, head, local_sem.at[4]),
    ]
    for load in loads:
        load.start()

    def peer_of(step):
        peer = lax.rem(me + step, n_all)
        return peer, lax.div(peer, n_vocab), lax.rem(peer, n_vocab)

    def along_dp(step):
        return lax.rem(d + step, n_dp)

    def along_vocab(step):
        return lax.rem(v + step, n_vocab)

    barrier = pltpu.get_barrier_semaphore()
    for step in range(1, n_dp):
        pl.semaphore_signal(barrier, inc=1, device_id={"dp": along_dp(step)}, device_id_type=MESH)
    for step in range(1, n_vocab):
        pl.semaphore_signal(barrier, inc=1, device_id={"vocab": along_vocab(step)}, device_id_type=MESH)
    pl.semaphore_wait(barrier, n_dp + n_vocab - 2)

    def att_copy(step):
        return pltpu.make_async_remote_copy(
            attention_hbm, attention_all.at[d], att_s.at[step], att_r.at[step],
            device_id={"dp": along_dp(step)}, device_id_type=MESH)

    def tok_copy(step):
        return pltpu.make_async_remote_copy(
            tokens_send.at[along_dp(step)], tokens_all.at[d], tok_s.at[step], tok_r.at[step],
            device_id={"dp": along_dp(step)}, device_id_type=MESH)

    for step in range(1, n_dp):
        att_copy(step).start()
    loads[1].wait()
    for block in range(n_dp):
        tokens_send[block] = tokens_own[:, block * wide : (block + 1) * wide]
    tokens_all[d] = tokens_send[d]

    for load in loads[4:7]:
        load.wait()

    slot_at = lax.broadcasted_iota(jnp.int32, (live, n_dp * slots), 1)
    row_at = lax.broadcasted_iota(jnp.int32, (live, n_dp * slots), 0)
    hit = jnp.zeros((live, n_dp * slots), jnp.bool_)
    start = jnp.int32(0)
    for block in range(n_dp):
        length = lengths_ref[block]
        place = slot_at - block * slots
        hit = hit | ((place >= 0) & (place < length) & (row_at == start + place))
        start = start + length
    pick = jnp.where(hit, 1.0, 0.0)
    pick_narrow = pick.astype(BF16)
    wanted = jnp.sum(pick * sampled_ref[...].astype(F32), axis=1, keepdims=True).astype(jnp.int32)

    gain_row = gain_ref[...].astype(F32).reshape(1, model)
    gain = jnp.zeros((1, wide), F32)
    for block in range(n_dp):
        gain = jnp.where(d == block, gain_row[:, block * wide : (block + 1) * wide], gain)

    loads[3].wait()
    tangent_narrow[...] = tangent[...].astype(BF16)
    loads[2].wait()
    loads[0].wait()
    for step in range(1, n_dp):
        att_copy(step).wait()
    for step in range(1, n_dp):
        tok_copy(step).start()
    everything = attention_all[...].reshape(n_dp * slots, attention_all.shape[2])
    packed = jnp.dot(pick_narrow, everything, preferred_element_type=F32).astype(BF16)
    packed_ref[...] = packed

    def chunk_copy(src, dst, send, recv):
        def copy(step):
            return pltpu.make_async_remote_copy(
                src.at[along_vocab(step)], dst.at[v], send.at[step], recv.at[step],
                device_id={"vocab": along_vocab(step)}, device_id_type=MESH)

        return copy

    hid_copy = chunk_copy(hid_send, hid_all, hid_s, hid_r)
    tan_copy = chunk_copy(tan_send, tan_all, tan_s, tan_r)
    hid_send[...] = jnp.dot(packed, projection[...], preferred_element_type=F32).reshape(n_vocab, ROWS, wide)
    for step in range(1, n_vocab):
        hid_copy(step).start()
    hid_all[v] = hid_send[v]
    tan_send[...] = jnp.dot(packed, tangent_narrow[...], preferred_element_type=F32).reshape(n_vocab, ROWS, wide)
    for step in range(1, n_vocab):
        tan_copy(step).start()
    tan_all[v] = tan_send[v]

    for step in range(1, n_dp):
        tok_copy(step).wait()
    my_slot = lax.broadcasted_iota(jnp.int32, (ROWS, live), 1)
    my_row = lax.broadcasted_iota(jnp.int32, (ROWS, live), 0) + v * ROWS
    own_rows = jnp.where(my_slot == my_row, 1.0, 0.0)
    own_pick = jnp.dot(own_rows.astype(BF16), pick_narrow, preferred_element_type=F32).astype(BF16)
    tokens = jnp.dot(
        own_pick, tokens_all[...].reshape(n_dp * slots, wide), preferred_element_type=F32
    )
    for step in range(1, n_vocab):
        hid_copy(step).wait()
    hidden = tokens + jnp.sum(hid_all[...], axis=0)
    for step in range(1, n_vocab):
        tan_copy(step).wait()
    tangent_hidden = jnp.sum(tan_all[...], axis=0)

    lane = lax.broadcasted_iota(jnp.int32, (ROWS, LANES), 1)
    squares = jnp.sum(hidden * hidden, axis=1, keepdims=True)
    cross = jnp.sum(hidden * tangent_hidden, axis=1, keepdims=True)
    norm_all[d] = jnp.where(lane < 1, squares, cross)

    def norm_copy(step):
        return pltpu.make_async_remote_copy(
            norm_all.at[d], norm_all.at[d], norm_s.at[step], norm_r.at[step],
            device_id={"dp": along_dp(step)}, device_id_type=MESH)

    for step in range(1, n_dp):
        norm_copy(step).start()
    for step in range(1, n_dp):
        norm_copy(step).wait()
    inverse = 1.0 / model
    means = jnp.sum(norm_all[...], axis=0) * inverse
    scale = lax.rsqrt(means[:, 0:1] + EPSILON)
    normed = gain * hidden * scale
    tangent_normed = gain * scale * (tangent_hidden - hidden * scale * scale * means[:, 1:2])
    msg_all[me] = jnp.concatenate([normed, tangent_normed], axis=0).astype(BF16)

    def to_all(src, dst, send, recv):
        def copy(step):
            _, pd, pv = peer_of(step)
            return pltpu.make_async_remote_copy(
                src(step), dst.at[me], send.at[step], recv.at[step],
                device_id={"dp": pd, "vocab": pv}, device_id_type=MESH)

        return copy

    def start_all(copy):
        if n_all <= 16:
            for step in range(1, n_all):
                copy(step).start()
        else:

            @pl.loop(1, n_all)
            def _(step):
                copy(step).start()

    def wait_all(copy):
        if n_all <= 16:
            for step in range(1, n_all):
                copy(step).wait()
        else:

            @pl.loop(1, n_all)
            def _(step):
                copy(step).wait()

    mate = v + 1 - 2 * lax.rem(v, 2)

    half = n_vocab // 2

    def msg_copy(far, step):
        slot = far * half + step
        return pltpu.make_async_remote_copy(
            msg_all.at[me], msg_all.at[me], msg_s.at[slot], msg_r.at[slot],
            device_id={"dp": along_dp(far), "vocab": along_vocab(2 * step)}, device_id_type=MESH)

    def pass_copy(far, step):
        slot = far * half + step
        came_from = along_dp(n_dp - far) * n_vocab + along_vocab(n_vocab - 2 * step)
        return pltpu.make_async_remote_copy(
            msg_all.at[came_from], msg_all.at[came_from], pass_s.at[slot], pass_r.at[slot],
            device_id={"vocab": mate}, device_id_type=MESH)

    hops = [(far, step) for far in range(n_dp) for step in range(half) if far + step > 0]
    for far, step in hops:
        msg_copy(far, step).start()
    pair = jnp.zeros((n_vocab * 2 * ROWS, columns), F32)
    for far in range(n_dp + 1):
        if far < n_dp:
            for step in range(half):
                if far + step > 0:
                    msg_copy(far, step).wait_recv()
                pass_copy(far, step).start()
        if far == 0:
            loads[7].wait()
            continue
        for step in range(half):
            pass_copy(far - 1, step).wait()
        block = along_dp(n_dp - far + 1)
        pair = pair + jnp.dot(
            msg_all[pl.ds(block * n_vocab, n_vocab)].reshape(n_vocab * 2 * ROWS, wide),
            head[pl.ds(pl.multiple_of(block * wide, 32), wide), :],
            preferred_element_type=F32,
        )
    for far, step in hops:
        msg_copy(far, step).wait_send()
    pair = pair.reshape(n_vocab, 2 * ROWS, columns)
    logits = pair[:, 0:ROWS].reshape(live, columns)
    squashed = jnp.tanh(logits * (1.0 / SOFT_CAP))
    slopes = 1.0 - squashed * squashed
    tangent_capped = slopes * pair[:, ROWS:].reshape(live, columns)
    exp_values = jnp.exp(SOFT_CAP * squashed)
    column_at = lax.broadcasted_iota(jnp.int32, (live, columns), 1) + me * columns
    total = jnp.sum(exp_values, axis=1, keepdims=True)
    weighted = jnp.sum(exp_values * tangent_capped, axis=1, keepdims=True)
    picked = jnp.sum(jnp.where(column_at == wanted, tangent_capped, 0.0), axis=1, keepdims=True)
    stat_lane = lax.broadcasted_iota(jnp.int32, (live, LANES), 1)
    stats = (
        jnp.where(stat_lane == 0, total, 0.0)
        + jnp.where(stat_lane == 1, weighted, 0.0)
        + jnp.where(stat_lane == 2, picked, 0.0)
    )
    if live < LANES:
        stats = jnp.concatenate([stats, jnp.zeros((LANES - live, LANES), F32)], axis=0)
    stat_all[me] = stats.T[0:ROWS]
    stat_copy = to_all(lambda step: stat_all.at[me], stat_all, stat_s, stat_r)
    start_all(stat_copy)
    wait_all(stat_copy)
    across = jnp.sum(stat_all[...], axis=0)
    across = jnp.concatenate([across, jnp.zeros((LANES - ROWS, LANES), F32)], axis=0).T[0:live]
    all_total = across[:, 0:1]
    tangent_mean = across[:, 1:2] / all_total
    token = across[:, 2:3] - tangent_mean
    token_row = lax.broadcasted_iota(jnp.int32, (live, slots // 2), 0)
    token_lane = lax.broadcasted_iota(jnp.int32, (live, slots // 2), 1) + d * (slots // 2)
    token_ref[...] = jnp.sum(jnp.where(token_row == token_lane, token, 0.0), axis=0, keepdims=True)

    back_logits = (exp_values / all_total * (tangent_capped - tangent_mean) * slopes).astype(BF16)
    inner_part = jnp.sum(back_logits.astype(F32) * logits, axis=1, keepdims=True)
    inner_tail = jnp.where(stat_lane == 0, inner_part, 0.0).reshape(n_vocab, ROWS, LANES)

    core = lax.rem(v, 2)

    def pair_copy(far, step):
        slot = far * half + step
        return pltpu.make_async_remote_copy(
            pair_send.at[far, 2 * step + 1 - core], pair_got.at[far, step], pair_s.at[slot], pair_r.at[slot],
            device_id={"vocab": mate}, device_id_type=MESH)

    def part_copy(far, step):
        slot = far * half + step
        return pltpu.make_async_remote_copy(
            part_send.at[slot], part_all.at[slot], part_s.at[slot], part_r.at[slot],
            device_id={"dp": along_dp(far), "vocab": along_vocab(2 * step)}, device_id_type=MESH)

    order = [*range(1, n_dp), 0]
    for turn in range(n_dp + 1):
        if turn < n_dp:
            far = order[turn]
            pair_send[far, :, :, 0:wide] = lax.dot_general(
                back_logits,
                head[pl.ds(pl.multiple_of(along_dp(far) * wide, 32), wide), :],
                NT,
                preferred_element_type=F32,
            ).reshape(n_vocab, ROWS, wide)
            pair_send[far, :, :, base:] = inner_tail
            for step in range(half):
                pair_copy(far, step).start()
        if turn == 0:
            continue
        far = order[turn - 1]
        for step in range(half):
            pair_copy(far, step).wait()
        for step in range(half):
            chunk = along_vocab(2 * step)
            got = pair_got[far, lax.div(chunk, 2)]
            added = pair_send[far, chunk, :, 0:wide] + got[:, 0:wide]
            tail = pair_send[far, chunk, :, base:] + got[:, base:]
            tail = tail[:, 0:1]
            high = tail.astype(BF16).astype(F32)
            middle = (tail - high).astype(BF16).astype(F32)
            tail = jnp.where(lane == 0, high, 0.0) + jnp.where(lane == 1, middle, 0.0) + jnp.where(
                lane == 2, tail - high - middle, 0.0
            )
            slot = far * half + step
            target = part_send if slot else part_all
            target[slot, :, 0:wide] = added.astype(BF16)
            target[slot, :, base:] = tail.astype(BF16)
            if slot:
                part_copy(far, step).start()
    for far, step in hops:
        part_copy(far, step).wait()
    back_gain = gain * jnp.sum(part_all[:, :, 0:wide].astype(F32), axis=0)
    inner_back = jnp.sum(jnp.sum(part_all[:, :, base:].astype(F32), axis=0), axis=1, keepdims=True) * inverse
    bh_all[v] = (scale * back_gain - hidden * (scale * scale * inner_back)).astype(BF16)

    def bh_copy(step):
        return pltpu.make_async_remote_copy(
            bh_all.at[v], bh_all.at[v], bh_s.at[step], bh_r.at[step],
            device_id={"vocab": along_vocab(step)}, device_id_type=MESH)

    for step in range(1, n_vocab):
        bh_copy(step).start()
    for step in range(1, n_vocab):
        bh_copy(step).wait()
    back_ref[...] = bh_all[...].astype(F32).reshape(live, wide).astype(BF16)


def local(n_dp, n_vocab, tokens_in, attention, out_projection, tangent, norm_gain, head_weight, lengths, sampled):
    slots, model = tokens_in.shape
    features, wide = out_projection.shape
    columns = head_weight.shape[1]
    live_dev = slots // 2
    live = live_dev * n_dp
    assert live == n_vocab * ROWS and live <= LANES
    n_all = n_dp * n_vocab
    padded = -(-wide // LANES) * LANES + LANES
    vmem, hbm = pl.BlockSpec(memory_space=pltpu.VMEM), pl.BlockSpec(memory_space=pltpu.HBM)
    dma = pltpu.SemaphoreType.DMA
    packed, back, token_mine = pl.pallas_call(
        functools.partial(fused_kernel, n_dp, n_vocab),
        out_shape=(
            pltpu.VMEM((live, features), BF16),
            pltpu.VMEM((live, wide), BF16),
            jax.ShapeDtypeStruct((1, live_dev), F32),
        ),
        in_specs=[hbm] * 8,
        out_specs=(vmem, vmem, vmem),
        scratch_shapes=[
            pltpu.SMEM(lengths.shape, jnp.int32),
            pltpu.VMEM((1, n_dp * slots), jnp.int32),
            pltpu.VMEM((model,), BF16),
            pltpu.VMEM((slots, model), BF16),
            pltpu.VMEM((n_dp, slots, wide), BF16),
            pltpu.VMEM((n_dp, slots, wide), BF16),
            pltpu.VMEM((n_dp, slots, features), BF16),
            pltpu.VMEM((features, wide), BF16),
            pltpu.VMEM((features, wide), F32),
            pltpu.VMEM((features, wide), BF16),
            pltpu.VMEM((model, columns), BF16),
            pltpu.VMEM((n_vocab, ROWS, wide), F32),
            pltpu.VMEM((n_vocab, ROWS, wide), F32),
            pltpu.VMEM((n_vocab, ROWS, wide), F32),
            pltpu.VMEM((n_vocab, ROWS, wide), F32),
            pltpu.VMEM((n_dp, ROWS, LANES), F32),
            pltpu.VMEM((n_all, 2 * ROWS, wide), BF16),
            pltpu.VMEM((n_all, ROWS, LANES), F32),
            pltpu.VMEM((n_dp, n_vocab, ROWS, padded), F32),
            pltpu.VMEM((n_dp, n_vocab // 2, ROWS, padded), F32),
            pltpu.VMEM((n_all // 2, ROWS, padded), BF16),
            pltpu.VMEM((n_all // 2, ROWS, padded), BF16),
            pltpu.VMEM((n_vocab, ROWS, wide), BF16),
            dma((8,)),
            dma((n_dp,)), dma((n_dp,)), dma((n_dp,)), dma((n_dp,)),
            dma((n_vocab,)), dma((n_vocab,)), dma((n_vocab,)), dma((n_vocab,)),
            dma((n_dp,)), dma((n_dp,)),
            dma((n_all // 2,)), dma((n_all // 2,)), dma((n_all // 2,)), dma((n_all // 2,)),
            dma((n_all,)), dma((n_all,)),
            dma((n_all // 2,)), dma((n_all // 2,)), dma((n_all // 2,)), dma((n_all // 2,)),
            dma((n_vocab,)), dma((n_vocab,)),
        ],
        compiler_params=pltpu.CompilerParams(
            collective_id=0, has_side_effects=True, vmem_limit_bytes=60 * 1024 * 1024
        ),
    )(lengths, sampled.reshape(1, -1), norm_gain,
      tokens_in, attention, out_projection, tangent, head_weight)
    fisher_product = lax.dot_general(packed, back, (((0,), (0,)), ((), ())), preferred_element_type=F32)
    return (fisher_product, token_mine.reshape(-1))


def solution(mesh):
    return jax.shard_map(
        functools.partial(local, mesh.shape["dp"], mesh.shape["vocab"]),
        mesh=mesh,
        in_specs=(
            P(("groups", "dp"), None),
            P(("groups", "dp"), "vocab"),
            P("vocab", "dp"),
            P(("groups", "vocab"), "dp"),
            P(),
            P(None, ("dp", "vocab")),
            P("groups"),
            P("groups"),
        ),
        out_specs=(P(("groups", "vocab"), "dp"), P(("groups", "dp"))),
        check_vma=False,
    )
```
